32 devices in a mesh: section: 4 (over y, x), dp: 8 (over z, core).
Axes of the slice: x: 2, y: 2, z: 4, core: 2. Of those that a mesh axis runs over, the one named last changes fastest.
Arguments:
- images_a: bfloat16 [64, 100, 384], P('dp'), may hold values from -6 to 6
- images_b: bfloat16 [64, 196, 384], P('dp'), may hold values from -6 to 6
- images_c: bfloat16 [64, 324, 384], P('dp'), may hold values from -6 to 6
- cotan_a: bfloat16 [64, 100, 384], P('dp'), may hold values from -6 to 6
- cotan_b: bfloat16 [64, 196, 384], P('dp'), may hold values from -6 to 6
- cotan_c: bfloat16 [64, 324, 384], P('dp'), may hold values from -6 to 6
- live_counts: int32 [32, 3], P('dp'), may hold values from 1 to 2, as said below
- scales: bfloat16 [2, 4, 384], replicated, may hold values from 0.25 to 1.75
- shifts: bfloat16 [2, 3, 384], replicated, may hold values from -3 to 3
- mix_a: bfloat16 [2, 100, 100], replicated, may hold values from -0.625 to 0.625
- mix_b: bfloat16 [2, 196, 196], replicated, may hold values from -0.4375 to 0.4375
- mix_c: bfloat16 [2, 324, 324], replicated, may hold values from -0.3125 to 0.3125
- patch_bias: bfloat16 [2, 620], replicated, may hold values from -3 to 3
- weight_in: bfloat16 [2, 384, 1536], replicated, may hold values from -0.3125 to 0.3125
- bias_in: bfloat16 [2, 1536], replicated, may hold values from -3 to 3
- weight_out: bfloat16 [2, 1536, 384], replicated, may hold values from -0.15625 to 0.15625
Outputs:
- output_a: bfloat16 [64, 100, 384], P(('dp', 'section'))
- output_b: bfloat16 [64, 196, 384], P(('dp', 'section'))
- output_c: bfloat16 [64, 324, 384], P(('dp', 'section'))
- grad_a: bfloat16 [64, 100, 384], P(('dp', 'section'))
- grad_b: bfloat16 [64, 196, 384], P(('dp', 'section'))
- grad_c: bfloat16 [64, 324, 384], P(('dp', 'section'))
- grad_scales: float32 [2, 4, 384], replicated
- grad_shifts: float32 [2, 3, 384], replicated
- grad_mix_a: float32 [2, 100, 100], replicated
- grad_mix_b: float32 [2, 196, 196], replicated
- grad_mix_c: float32 [2, 324, 324], replicated
- grad_patch_bias: float32 [2, 620], replicated
- grad_weight_in: float32 [2, 384, 1536], replicated
- grad_bias_in: float32 [2, 1536], replicated
- grad_weight_out: float32 [2, 1536, 384], replicated
The draws below stay inside these ranges and needn't reach their ends.
Inputs may be any that keep to these rules, and one draw needn't show every extreme that they name: `live_counts`: live images of one size in one micro-batch; some entry is 2 and some is 1.
All inputs are finite; a program needn't handle non-finite values.
Results may differ from the reference program's by a relative error of at most 0.015.
Values may be sent and summed in bfloat16 or wider, within the bound.
A program may use at most 256 MiB of HBM per device.

```python
import jax
import jax.numpy as jnp
from jax import lax

D = 384
HID = 1536
PATCH_A = 100
PATCH_B = 196
PATCH_C = 324
LAYERS = 2
CAP = 2
PATCHES = 620
BATCHES = 32
IMAGES = 64


def draw_live_counts(key, part):
    key = jax.random.fold_in(key, 7)
    keys = jax.random.split(key, 4)
    counts = jax.random.randint(keys[0], (BATCHES, 3), 1, CAP + 1)
    row_pick = jax.random.randint(keys[1], (), 0, BATCHES)
    col_pick = jax.random.randint(keys[2], (), 0, 3)
    other_row = (row_pick + 1 + jax.random.randint(keys[3], (), 0, BATCHES - 1)) % BATCHES
    counts = counts.at[row_pick, col_pick].set(CAP)
    counts = counts.at[other_row, col_pick].set(1)
    return counts.astype(jnp.int32)


def block_scale(own_key, dims, pieces, least, high):
    gain, own = 1.0, jax.random.fold_in(own_key, 6)
    for position, parts in pieces:
        draws = jnp.exp(jax.random.uniform(jax.random.fold_in(own, position), (parts,), jnp.float32, least / len(pieces), high / len(pieces)))
        gain = gain * jnp.repeat(draws, dims[position] // parts).reshape([-1 if axis == position else 1 for axis in range(len(dims))])
    return gain


def centred(own_key, shape, scale, most, shards=(), kind=jnp.bfloat16):
    factor_of = block_scale(own_key, shape, shards, -0.22, 0.18) if shards else 1.0
    entries = jax.random.normal(own_key, shape, jnp.float32) * scale * factor_of
    return jnp.minimum(jnp.maximum(entries, -most), most).astype(kind)


def setup_inputs(seed: int = 0) -> dict:
    arg_keys = jax.random.split(jax.random.key(seed), 17)
    return {
        "images_a": centred(arg_keys[0], (IMAGES, PATCH_A, D), 1.0, 6.0, ((0, 8),)),
        "images_b": centred(arg_keys[1], (IMAGES, PATCH_B, D), 1.0, 6.0, ((0, 8),)),
        "images_c": centred(arg_keys[2], (IMAGES, PATCH_C, D), 1.0, 6.0, ((0, 8),)),
        "cotan_a": centred(arg_keys[3], (IMAGES, PATCH_A, D), 1.0, 6.0, ((0, 8),)),
        "cotan_b": centred(arg_keys[4], (IMAGES, PATCH_B, D), 1.0, 6.0, ((0, 8),)),
        "cotan_c": centred(arg_keys[5], (IMAGES, PATCH_C, D), 1.0, 6.0, ((0, 8),)),
        "live_counts": draw_live_counts(jax.random.fold_in(arg_keys[16], 71), 0),
        "scales": jnp.clip(1.0 + 0.15 * jax.random.normal(arg_keys[7], (LAYERS, 4, D), jnp.float32), 0.25, 1.75).astype(jnp.bfloat16),
        "shifts": centred(arg_keys[8], (LAYERS, 3, D), 0.3, 3.0),
        "mix_a": centred(arg_keys[9], (LAYERS, PATCH_A, PATCH_A), PATCH_A ** -0.5, 0.625),
        "mix_b": centred(arg_keys[10], (LAYERS, PATCH_B, PATCH_B), PATCH_B ** -0.5, 0.4375),
        "mix_c": centred(arg_keys[11], (LAYERS, PATCH_C, PATCH_C), PATCH_C ** -0.5, 0.3125),
        "patch_bias": centred(arg_keys[12], (LAYERS, PATCHES), 0.3, 3.0),
        "weight_in": centred(arg_keys[13], (LAYERS, D, HID), D ** -0.5, 0.3125),
        "bias_in": centred(arg_keys[14], (LAYERS, HID), 0.3, 3.0),
        "weight_out": centred(arg_keys[15], (LAYERS, HID, D), HID ** -0.5, 0.15625),
    }


@jax.custom_vjp
def low(v):
    return lax.optimization_barrier(v.astype(jnp.bfloat16)).astype(jnp.float32)

@jax.custom_vjp
def low_back(v):
    return v

def low_keep(v):
    return (low(v), None)

def low_pass(kept, grad):
    return (grad,)

def back_keep(v):
    return (v, None)

def back_low(kept, grad):
    return (low(grad),)
low.defvjp(low_keep, low_pass)
low_back.defvjp(back_keep, back_low)
precise = lax.Precision.HIGHEST

def cross_patch(inputs, gain_vec, shift_vec, layer_scale, matrices, biases):
    results = []
    for source, matrix, offset in zip(inputs, matrices, biases):
        source = low_back(source)
        normed = low(gain_vec * source + shift_vec)
        product = low_back(jnp.einsum('pq,iqd->ipd', matrix, normed, precision=precise))
        results.append(low(source + layer_scale * (product + offset[None, :, None])))
    return results

def channel_mlp(inputs, gain_vec, shift_vec, layer_scale, first_weight, first_bias, second_weight, second_bias):
    shapes_in = [member.shape for member in inputs]
    joined = jnp.concatenate([low_back(member).reshape(-1, member.shape[-1]) for member in inputs], axis=0)
    normed = low(gain_vec * joined + shift_vec)
    pre_act = low_back(jnp.dot(normed, first_weight, precision=precise)) + first_bias
    hidden = low(jax.nn.gelu(pre_act, approximate=False))
    branch = low_back(jnp.dot(hidden, second_weight, precision=precise)) + second_bias
    merged = low(joined + layer_scale * branch)
    results = []
    row_start = 0
    for member_shape in shapes_in:
        row_count = member_shape[0] * member_shape[1]
        results.append(merged[row_start:row_start + row_count].reshape(member_shape))
        row_start += row_count
    return results

def network(params, inputs):
    scales, shifts, mix_a, mix_b, mix_c, patch_bias, weight_in, bias_in, weight_out = params
    states = list(inputs)
    for layer_no in range(LAYERS):
        offsets = [patch_bias[layer_no, :PATCH_A], patch_bias[layer_no, PATCH_A:PATCH_A + PATCH_B], patch_bias[layer_no, PATCH_A + PATCH_B:]]
        states = cross_patch(states, scales[layer_no, 0], shifts[layer_no, 0], scales[layer_no, 1], [mix_a[layer_no], mix_b[layer_no], mix_c[layer_no]], offsets)
        states = channel_mlp(states, scales[layer_no, 2], shifts[layer_no, 1], scales[layer_no, 3], weight_in[layer_no], bias_in[layer_no], weight_out[layer_no], shifts[layer_no, 2])
    return tuple(states)

def reference(images_a, images_b, images_c, cotan_a, cotan_b, cotan_c, live_counts, scales, shifts, mix_a, mix_b, mix_c, patch_bias, weight_in, bias_in, weight_out):
    params = tuple((member.astype(jnp.float32) for member in (scales, shifts, mix_a, mix_b, mix_c, patch_bias, weight_in, bias_in, weight_out)))
    widths = (PATCH_A, PATCH_B, PATCH_C)

    def as_batches(array, width):
        return array.astype(jnp.float32).reshape(BATCHES, CAP, width, D)
    inputs = tuple((as_batches(array, width) for array, width in zip((images_a, images_b, images_c), widths)))
    cotans = tuple((as_batches(array, width) for array, width in zip((cotan_a, cotan_b, cotan_c), widths)))

    def one_batch(totals, batch_in):
        members, cotangents, counts = batch_in
        slot_ids = jnp.arange(CAP, dtype=jnp.int32)
        live_masks = tuple(((slot_ids < counts[kind_no]).astype(jnp.float32)[:, None, None] for kind_no in range(3)))
        outputs, pullback = jax.vjp(network, params, members)
        grads_params, grads_inputs = pullback(tuple((mask_one * cot_one for mask_one, cot_one in zip(live_masks, cotangents))))
        totals = jax.tree.map(jnp.add, totals, grads_params)
        shown = tuple(((mask_one * out_one).astype(jnp.bfloat16) for mask_one, out_one in zip(live_masks, outputs)))
        backs = tuple((grad_one.astype(jnp.bfloat16) for grad_one in grads_inputs))
        return (totals, (shown, backs))
    empty_grads = jax.tree.map(jnp.zeros_like, params)
    totals, (shown, backs) = lax.scan(one_batch, empty_grads, (inputs, cotans, live_counts))
    flat_out = tuple((array.reshape(IMAGES, width, D) for array, width in zip(shown, widths)))
    flat_back = tuple((array.reshape(IMAGES, width, D) for array, width in zip(backs, widths)))
    return (flat_out[0], flat_out[1], flat_out[2], flat_back[0], flat_back[1], flat_back[2], totals[0], totals[1], totals[2], totals[3], totals[4], totals[5], totals[6], totals[7], totals[8])
```

```python
import functools

import jax
import jax.numpy as jnp
from jax import lax
from jax.experimental import pallas as pl
from jax.experimental.pallas import tpu as pltpu
from jax.sharding import PartitionSpec as P

MESH = pl.DeviceIdType.MESH
f32 = jnp.float32
bf16 = jnp.bfloat16
LAYERS = 2
KINDS = 3
LANES = 128
ROWS = 16
CHUNK = 256
SLACK = 2
BLOCK = 32
HALF_LOG2E = -0.7213475204444817
HALF_ROOT = 0.7071067811865476
PDF_SCALE = 0.3989422804014327


def up(value, unit):
    return -(-value // unit) * unit


def nt(left, right):
    return lax.dot_general(left, right, (((1,), (1,)), ((), ())), preferred_element_type=f32)


def nn(left, right):
    return jnp.dot(left, right, preferred_element_type=f32)


def col_sum(value):
    return jnp.sum(value, axis=0, keepdims=True)


def cuts(total, pieces):
    tiles = total // ROWS
    marks = [tiles * k // pieces * ROWS for k in range(pieces + 1)]
    return [(marks[k], marks[k + 1] - marks[k]) for k in range(pieces)]


class Plan:
    def __init__(self, sections, dp, slots, widths, chans, hid):
        self.sections, self.dp, self.slots, self.widths, self.chans, self.hid = sections, dp, slots, widths, chans, hid
        self.padded = tuple(up(width + 1, ROWS) for width in widths)
        self.wide = tuple(up(rows, LANES) for rows in self.padded)
        self.segments = []
        start = 0
        for kind in range(KINDS):
            for slot in range(slots):
                self.segments.append((kind, slot, start))
                start += self.padded[kind]
        self.rows = start
        self.chunks = hid // CHUNK
        self.steps = self.chunks + 1
        self.pieces = LAYERS * self.steps
        self.depth = min(4, dp // 2)
        self.outer = dp // (2 * self.depth)
        self.size = 2 * chans * CHUNK // LANES
        self.half, self.quarter, self.eighth = self.size // 2, self.size // 4, self.size // 8
        self.last = self.eighth // self.depth
        self.places, place = {}, 0
        for kind in reversed(range(KINDS)):
            self.places[kind] = place
            place += self.padded[kind] * (self.wide[kind] // LANES)
        assert place <= self.size and self.last % ROWS == 0 and sections == 4 and self.depth > 1


def kernel(
    plan,
    xa, xb, xc, ca, cb, cc, counts, scales, shifts, mix_a, mix_b, mix_c, patch_bias, bias_in, w_in_hbm, w_out_hbm,
    oa, ob, oc, ga, gb, gc, result,
    w_in, w_out, pad, pbias, aff, bias32, mat_a, mat_b, mat_c, tam_a, tam_b, tam_c,
    xs, x1s, us, hs, ds, z2, acc, grad, dvr, dvt, z2t, da, vecs, bgrad,
    own, land0, land1, land2, land3,
    io_sem, send_sem, recv_sem,
):
    widths, padded, wide = plan.widths, plan.padded, plan.wide
    slots, chans, rows = plan.slots, plan.chans, plan.rows
    section = lax.axis_index("section")
    dp = lax.axis_index("dp")
    core = lax.rem(dp, 2)
    deep = lax.rem(lax.div(dp, 2), plan.depth)
    block = dp - lax.rem(dp, 2 * plan.depth)
    bit0, bit1 = lax.rem(section, 2), lax.div(section, 2)
    first = jnp.where(core == 0, bit0, bit1)
    second = jnp.where(core == 0, bit1, bit0)
    flip0 = section + 1 - 2 * bit0
    flip1 = section + 2 - 4 * bit1
    first_to = (jnp.where(core == 0, flip0, flip1), dp)
    second_to = (jnp.where(core == 0, flip1, flip0), dp)
    core_to = (section, dp + 1 - 2 * core)

    def deep_to(step):
        return (section, block + lax.rem(deep + step, plan.depth) * 2 + core)

    partners = [core_to, first_to, second_to] + [deep_to(step) for step in range(1, plan.depth)]
    barrier = pltpu.get_barrier_semaphore()
    for partner in partners:
        pl.semaphore_signal(barrier, inc=1, device_id=partner, device_id_type=MESH)

    raw_x, raw_c = (oa, ob, oc), (ga, gb, gc)
    fetches = []
    mine = pl.ds(pl.multiple_of(section * slots, slots), slots)
    pairs = list(zip((xa, xb, xc), raw_x)) + list(zip((ca, cb, cc), raw_c))
    for place, (source, target) in enumerate(pairs):
        fetches.append(pltpu.make_async_copy(source.at[:, mine, :], target, io_sem.at[place]))
    fetches.append(pltpu.make_async_copy(w_in_hbm, w_in, io_sem.at[6]))
    fetches.append(pltpu.make_async_copy(w_out_hbm, w_out, io_sem.at[7]))
    for fetch in fetches[:3] + fetches[6:] + fetches[3:6]:
        fetch.start()

    for layer in range(LAYERS):
        aff[layer, 0:4, :] = scales[layer].astype(f32)
        aff[layer, 4:7, :] = shifts[:, layer, :].astype(f32)
        bias32[layer, :, :] = bias_in[...].astype(f32)[layer : layer + 1]
    pbias[...] = jnp.zeros_like(pbias)
    pbias[0:LAYERS, 0 : patch_bias.shape[1]] = patch_bias[...].astype(f32)
    pad[...] = jnp.zeros_like(pad)

    mats, tams = (mat_a, mat_b, mat_c), (tam_a, tam_b, tam_c)
    offset = 0
    for kind, source in enumerate((mix_a, mix_b, mix_c)):
        width, rows_k, size = widths[kind], padded[kind], wide[kind]
        turned = pltpu.roll(pbias[...], pbias.shape[1] - offset, 1) if offset else pbias[...]
        offset += width
        row = lax.broadcasted_iota(jnp.int32, (size, size), 0)
        col = lax.broadcasted_iota(jnp.int32, (size, size), 1)
        for layer in range(LAYERS):
            pad[0:size, 0:size] = jnp.zeros((size, size), f32)
            pad[0:width, 0:width] = source[:, layer, :].astype(f32)
            biases = turned[layer : layer + 1, 0:size]
            column = jnp.sum(jnp.where(row == col, biases, 0.0), axis=1, keepdims=True)
            whole = jnp.where((col == width) & (row < width), column, pad[0:size, 0:size])
            mats[kind][layer] = whole[0:rows_k, 0:rows_k].astype(bf16)
            tams[kind][layer] = whole.T[0:rows_k, 0:rows_k].astype(bf16)

    def padded_image(value, kind):
        width, rows_k = widths[kind], padded[kind]
        edge = width // 8 * 8
        pad[edge:rows_k, :] = jnp.zeros((rows_k - edge, chans), f32)
        pad[0:width, :] = value
        return pad[0:rows_k, :]

    def live(kind, slot):
        return (slot < counts[section, kind]).astype(f32)

    for kind, slot, start in plan.segments:
        if slot == 0:
            fetches[kind].wait()
        xs[0, pl.ds(start, padded[kind]), :] = padded_image(raw_x[kind][:, slot, :].astype(f32), kind).astype(bf16)

    def ones_row(kind, value):
        row = lax.broadcasted_iota(jnp.int32, value.shape, 0)
        return jnp.where(row == widths[kind], 1.0, value).astype(bf16)

    def forward(layer):
        vec = aff[layer]
        for kind, slot, start in plan.segments:
            span = pl.ds(start, padded[kind])
            x = xs[layer, span, :].astype(f32)
            z = ones_row(kind, vec[0:1] * x + vec[4:5])
            p = nn(mats[kind][layer], z)
            us[layer, span, :] = p.astype(bf16)
            x1 = (x + vec[1:2] * p).astype(bf16)
            x1s[layer, span, :] = x1
            z2[span, :] = (vec[2:3] * x1.astype(f32) + vec[5:6]).astype(bf16)
            if layer < LAYERS - 1:
                acc[span, :] = jnp.broadcast_to(vec[6:7], (padded[kind], chans))

        if layer == 0:
            fetches[6].wait()
            fetches[7].wait()

        for chunk in range(plan.chunks):
            lanes = pl.ds(chunk * CHUNK, CHUNK)
            bias = bias32[layer, :, lanes]
            first_weight = w_in[layer, :, lanes]
            second_weight = w_out[layer, lanes, :]
            for start, size in cuts(rows, 2):
                span = pl.ds(start, size)
                product = nn(z2[span, :], first_weight)
                for low in range(0, size, BLOCK):
                    high = min(low + BLOCK, size)
                    a = product[low:high] + bias
                    cdf = 0.5 + 0.5 * lax.erf(a * HALF_ROOT)
                    slope = a * jnp.exp2(a * a * HALF_LOG2E) * PDF_SCALE
                    block_span = pl.ds(start + low, high - low)
                    hs[layer, chunk, block_span, :] = (a * cdf).astype(bf16)
                    ds[layer, chunk, block_span, :] = (cdf + slope).astype(bf16)
                if layer < LAYERS - 1:
                    acc[span, :] += nn(hs[layer, chunk, span, :], second_weight)

        if layer < LAYERS - 1:
            for kind, slot, start in plan.segments:
                span = pl.ds(start, padded[kind])
                xs[layer + 1, span, :] = (x1s[layer, span, :].astype(f32) + vec[3:4] * acc[span, :]).astype(bf16)

    for layer in range(LAYERS):
        forward(layer)

    for kind, slot, start in plan.segments:
        if slot == 0:
            fetches[KINDS + kind].wait()
        cot = raw_c[kind][:, slot, :].astype(f32) * live(kind, slot)
        grad[pl.ds(start, padded[kind]), :] = padded_image(cot, kind).astype(bf16)

    pl.semaphore_wait(barrier, len(partners))

    base0 = core * plan.half
    base1 = base0 + first * plan.quarter
    base2 = base1 + second * plan.eighth
    base3 = base2 + deep * plan.last

    def at(ref, piece, start, size):
        return ref.at[piece, pl.ds(pl.multiple_of(start, ROWS), size)]

    def send(piece, hop, source, target, to):
        return pltpu.make_async_remote_copy(
            src_ref=source,
            dst_ref=target,
            send_sem=send_sem.at[hop],
            recv_sem=recv_sem.at[piece, hop],
            device_id=to,
            device_id_type=MESH,
        )

    def hop0(piece):
        return [send(piece, 0, at(own, piece, (1 - core) * plan.half, plan.half), land0.at[piece], core_to)]

    def hop1(piece):
        return [send(piece, 1, at(land0, piece, (1 - first) * plan.quarter, plan.quarter), land1.at[piece], first_to)]

    def hop2(piece):
        return [send(piece, 2, at(land1, piece, (1 - second) * plan.eighth, plan.eighth), land2.at[piece], second_to)]

    def hop3(piece):
        return [
            send(
                piece,
                3,
                at(land2, piece, lax.rem(deep + step, plan.depth) * plan.last, plan.last),
                land3.at[piece, step - 1],
                deep_to(step),
            )
            for step in range(1, plan.depth)
        ]

    def hop4(piece):
        spot = at(result, piece, base3, plan.last)
        return [send(piece, 4, spot, spot, deep_to(step)) for step in range(1, plan.depth)]

    def hop5(piece):
        spot = at(result, piece, base2, plan.eighth)
        return [send(piece, 5, spot, spot, second_to)]

    def hop6(piece):
        spot = at(result, piece, base1, plan.quarter)
        return [send(piece, 6, spot, spot, first_to)]

    def hop7(piece):
        spot = at(result, piece, base0, plan.half)
        return [send(piece, 7, spot, spot, core_to)]

    others = plan.last * (plan.depth - 1)

    def brought(piece, hop):
        whole = [
            land0.at[piece],
            land1.at[piece],
            land2.at[piece],
            land3.at[piece],
            at(result, piece, base2, others),
            at(result, piece, base2, plan.eighth),
            at(result, piece, base1, plan.quarter),
            at(result, piece, base0, plan.half),
        ][hop]
        return send(piece, hop, whole, whole, core_to)

    totals = [land0, land1, land2, land3, land3, land2, land1, land0]

    def start(copies):
        for copy in copies:
            copy.start()

    def get(ref, piece, start, size):
        return ref[piece, pl.ds(pl.multiple_of(start, ROWS), size), :].astype(f32)

    def add0(piece):
        land0[piece] = (land0[piece].astype(f32) + get(own, piece, base0, plan.half)).astype(bf16)

    def add1(piece):
        land1[piece] = (land1[piece].astype(f32) + get(land0, piece, first * plan.quarter, plan.quarter)).astype(bf16)

    def add2(piece):
        land2[piece] = (land2[piece].astype(f32) + get(land1, piece, second * plan.eighth, plan.eighth)).astype(bf16)

    def add3(piece):
        total = get(land2, piece, deep * plan.last, plan.last)
        for step in range(plan.depth - 1):
            total = total + land3[piece, step].astype(f32)
        result[piece, pl.ds(pl.multiple_of(base3, ROWS), plan.last), :] = total.astype(bf16)

    def nothing(piece):
        pass

    hops = [hop0, hop1, hop2, hop3, hop4, hop5, hop6, hop7]
    adds = [add0, add1, add2, add3, nothing, nothing, nothing, nothing]

    def tick(moment):
        for stage in range(len(hops) + 1):
            piece = moment - SLACK * stage

            @pl.when((piece >= 0) & (piece < plan.pieces))
            def _(stage=stage, piece=piece):
                if stage > 0:
                    brought(piece, stage - 1).wait_recv()
                    adds[stage - 1](piece)
                if stage < len(hops):
                    start(hops[stage](piece))

    def backward(turn):
        layer = LAYERS - 1 - turn
        vec = aff[layer]
        bias_sum = jnp.zeros((1, chans), f32)
        vecs[...] = jnp.zeros_like(vecs)
        for start in range(0, rows, LANES):
            span = pl.ds(start, min(LANES, rows - start))
            g = grad[span, :].astype(f32)
            dv = vec[3:4] * g
            bias_sum = bias_sum + col_sum(dv)
            low = dv.astype(bf16)
            dvr[span, :] = low
            dvt[:, span] = low.T
            z2t[:, span] = (vec[2:3] * x1s[layer, span, :].astype(f32) + vec[5:6]).astype(bf16).T
            acc[span, :] = jnp.zeros((span.size, chans), f32)

        def step(chunk, carry):
            lanes = pl.ds(pl.multiple_of(chunk * CHUNK, CHUNK), CHUNK)
            first_weight = w_in[layer, :, lanes]
            second_weight = w_out[layer, lanes, :]
            total = jnp.zeros((8, CHUNK), f32)
            for start, size in cuts(rows, 1):
                span = pl.ds(start, size)
                dh = nt(dvr[span, :], second_weight)
                for low in range(0, size, BLOCK):
                    high = min(low + BLOCK, size)
                    block_span = pl.ds(start + low, high - low)
                    dact = dh[low:high] * ds[layer, chunk, block_span, :].astype(f32)
                    total = total + dact.reshape(-1, 8, CHUNK).sum(axis=0)
                    da[block_span, :] = dact.astype(bf16)
                acc[span, :] += nt(da[span, :], first_weight)
            bgrad[:, lanes] = col_sum(total)
            piece = turn * plan.steps + chunk
            gin = nn(z2t[...], da[...]).astype(bf16)
            for part in range(CHUNK // LANES):
                own[piece, pl.ds(part * chans, chans), :] = gin[:, part * LANES : (part + 1) * LANES]
            gout = nn(dvt[...], hs[layer, chunk]).astype(bf16).T
            vecs[...] += (gout.astype(f32) * second_weight.astype(f32)).reshape(-1, 8, chans).sum(axis=0)
            for part in range(chans // LANES):
                own[piece, pl.ds(plan.half + part * CHUNK, CHUNK), :] = gout[:, part * LANES : (part + 1) * LANES]
            tick(piece)
            return carry

        lax.fori_loop(0, plan.chunks, step, 0)

        piece = turn * plan.steps + plan.chunks
        sums = [jnp.zeros((1, chans), f32) for _ in range(5)]
        for kind in range(KINDS):
            width, rows_k, size = widths[kind], padded[kind], wide[kind]
            mix_grad = jnp.zeros((rows_k, rows_k), f32)
            for seg_kind, slot, start in plan.segments:
                if seg_kind != kind:
                    continue
                span = pl.ds(start, rows_k)
                dz2 = acc[span, :]
                sums[3] = sums[3] + col_sum(x1s[layer, span, :].astype(f32) * dz2)
                sums[4] = sums[4] + col_sum(dz2)
                g1 = (grad[span, :].astype(f32) + vec[2:3] * dz2).astype(bf16).astype(f32)
                sums[2] = sums[2] + col_sum(g1 * us[layer, span, :].astype(f32))
                dp = (vec[1:2] * g1).astype(bf16)
                x = xs[layer, span, :].astype(f32)
                z = ones_row(kind, vec[0:1] * x + vec[4:5])
                mix_grad = mix_grad + nt(dp, z)
                dz = nn(tams[kind][layer], dp)
                row = lax.broadcasted_iota(jnp.int32, dz.shape, 0)
                dz = jnp.where(row < width, dz, 0.0)
                sums[0] = sums[0] + col_sum(x * dz)
                sums[1] = sums[1] + col_sum(dz)
                grad[span, :] = (g1 + vec[0:1] * dz).astype(bf16)
            pad[0:rows_k, 0:rows_k] = mix_grad
            if kind == KINDS - 1:
                for place in range(5):
                    pad[width + place : width + place + 1, :] = sums[place]
                pad[width + 5 : width + 6, :] = (col_sum(vecs[...]) + vec[6:7] * bias_sum) / vec[3:4]
                pad[width + 6 : width + 7, :] = bias_sum
                for place in range(plan.hid // chans):
                    spot = width + 7 + place
                    pad[spot : spot + 1, :] = bgrad[:, place * chans : (place + 1) * chans]
            for part in range(size // LANES):
                place = plan.places[kind] + part * rows_k
                own[piece, pl.ds(place, rows_k), :] = pad[0:rows_k, part * LANES : (part + 1) * LANES].astype(bf16)
        tick(piece)

    for turn in range(LAYERS):
        backward(turn)

    def shown(buffer, kind, slot, start):
        return buffer[pl.ds(start, padded[kind]), :].astype(f32)[0 : widths[kind]]

    acc[...] = jnp.zeros_like(acc)

    def drain(moment, carry):
        tick(moment)

        @pl.when(moment == plan.pieces)
        def _():
            for kind, slot, begin in plan.segments:
                raw_c[kind][:, slot, :] = shown(grad, kind, slot, begin).astype(bf16)

        @pl.when(moment < plan.pieces + plan.chunks)
        def _():
            chunk = moment - plan.pieces
            lanes = pl.ds(pl.multiple_of(chunk * CHUNK, CHUNK), CHUNK)
            acc[...] += nn(hs[LAYERS - 1, chunk], w_out[LAYERS - 1, lanes, :])

        @pl.when(moment == plan.pieces + plan.chunks)
        def _():
            vec = aff[LAYERS - 1]
            for kind, slot, begin in plan.segments:
                span = pl.ds(begin, padded[kind])
                y = (x1s[LAYERS - 1, span, :].astype(f32) + vec[3:4] * (acc[span, :] + vec[6:7])).astype(bf16)
                raw_x[kind][:, slot, :] = (y.astype(f32) * live(kind, slot)).astype(bf16)[0 : widths[kind]]

        return carry

    lax.fori_loop(plan.pieces, plan.pieces + SLACK * len(hops), drain, 0)

    for hop, total in enumerate(totals):
        pltpu.make_async_remote_copy(
            src_ref=total,
            dst_ref=total,
            send_sem=send_sem.at[hop],
            recv_sem=recv_sem.at[0, hop],
            device_id=core_to,
            device_id_type=MESH,
        ).wait_send()


def body(plan, *args):
    slots, chans, hid, rows = plan.slots, plan.chans, plan.hid, plan.rows
    images = [(width, slots, chans) for width in plan.widths]
    anywhere = pl.BlockSpec(memory_space=pl.ANY)
    vmem = pl.BlockSpec(memory_space=pltpu.VMEM)
    in_specs = [anywhere] * 6 + [pl.BlockSpec(memory_space=pltpu.SMEM)] + [vmem] * 7 + [anywhere] * 2
    (
        *pictures,
        live_counts,
        scales,
        shifts,
        mix_a,
        mix_b,
        mix_c,
        patch_bias,
        weight_in,
        bias_in,
        weight_out,
    ) = args
    scratch = [
        pltpu.VMEM((LAYERS, chans, hid), bf16),
        pltpu.VMEM((LAYERS, hid, chans), bf16),
        pltpu.VMEM((max(plan.wide), chans), f32),
        pltpu.VMEM((8, up(patch_bias.shape[1], LANES)), f32),
        pltpu.VMEM((LAYERS, 8, chans), f32),
        pltpu.VMEM((LAYERS, 1, hid), f32),
    ]
    scratch += [pltpu.VMEM((LAYERS, size, size), bf16) for size in plan.padded * 2]
    scratch += [
        pltpu.VMEM((LAYERS, rows, chans), bf16),
        pltpu.VMEM((LAYERS, rows, chans), bf16),
        pltpu.VMEM((LAYERS, rows, chans), bf16),
        pltpu.VMEM((LAYERS, plan.chunks, rows, CHUNK), bf16),
        pltpu.VMEM((LAYERS, plan.chunks, rows, CHUNK), bf16),
        pltpu.VMEM((rows, chans), bf16),
        pltpu.VMEM((rows, chans), f32),
        pltpu.VMEM((rows, chans), bf16),
        pltpu.VMEM((rows, chans), bf16),
        pltpu.VMEM((chans, rows), bf16),
        pltpu.VMEM((chans, rows), bf16),
        pltpu.VMEM((rows, CHUNK), bf16),
        pltpu.VMEM((8, chans), f32),
        pltpu.VMEM((1, hid), f32),
        pltpu.VMEM((plan.pieces, plan.size, LANES), bf16),
        pltpu.VMEM((plan.pieces, plan.half, LANES), bf16),
        pltpu.VMEM((plan.pieces, plan.quarter, LANES), bf16),
        pltpu.VMEM((plan.pieces, plan.eighth, LANES), bf16),
        pltpu.VMEM((plan.pieces, plan.depth - 1, plan.last, LANES), bf16),
        pltpu.SemaphoreType.DMA((8,)),
        pltpu.SemaphoreType.DMA((8,)),
        pltpu.SemaphoreType.DMA((plan.pieces, 8)),
    ]
    out_shape = [pltpu.VMEM(shape, bf16) for shape in images * 2]
    stays = pltpu.VMEM if plan.outer == 1 else jax.ShapeDtypeStruct
    out_shape.append(stays((plan.pieces, plan.size, LANES), bf16))
    views = [picture.transpose(1, 0, 2) for picture in pictures]
    mixes = [mix.transpose(1, 0, 2) for mix in (mix_a, mix_b, mix_c)]
    *shown, sums = pl.pallas_call(
        functools.partial(kernel, plan),
        out_shape=out_shape,
        in_specs=in_specs,
        out_specs=[vmem] * 7,
        scratch_shapes=scratch,
        compiler_params=pltpu.CompilerParams(
            collective_id=0, has_side_effects=True, vmem_limit_bytes=(55 if plan.outer == 1 else 60) * 1024 * 1024
        ),
    )(*views, live_counts, scales, shifts.transpose(1, 0, 2), *mixes, patch_bias, bias_in, weight_in, weight_out)
    if plan.outer > 1:
        ring = 2 * plan.depth
        groups = [[low + ring * high for high in range(plan.outer)] for low in range(ring)]
        sums = lax.psum(sums, "dp", axis_index_groups=groups)
    finals = [jax.ShapeDtypeStruct(shape, bf16) for shape in images * 2]
    finals += [
        jax.ShapeDtypeStruct(shape, f32)
        for shape in [(LAYERS, 4, chans), (3, LAYERS, chans)]
        + [(width, LAYERS, width) for width in plan.widths]
        + [(LAYERS, sum(plan.widths)), (LAYERS, chans, hid), (LAYERS, hid), (LAYERS, hid, chans)]
    ]
    out = pl.pallas_call(
        functools.partial(unpack, plan),
        out_shape=finals,
        in_specs=[vmem] * 7,
        out_specs=[anywhere] * 6 + [vmem] * 6 + [anywhere, vmem, anywhere],
        scratch_shapes=[
            pltpu.VMEM((LAYERS, chans, hid), f32),
            pltpu.VMEM((LAYERS, hid, chans), f32),
            pltpu.VMEM((max(plan.wide), chans), f32),
            pltpu.SemaphoreType.DMA((6,)),
            pltpu.SemaphoreType.DMA((LAYERS, plan.chunks, 2)),
        ],
        compiler_params=pltpu.CompilerParams(vmem_limit_bytes=24 * 1024 * 1024),
    )(*shown, sums)
    order = [value.transpose(1, 0, 2) for value in out[:6]]
    return (*order, out[6], out[7].transpose(1, 0, 2), *(mix.transpose(1, 0, 2) for mix in out[8:11]), *out[11:])


def unpack(
    plan, ia, ib, ic, ja, jb, jc, held,
    oa, ob, oc, ga, gb, gc, g_scales, g_shifts, g_mix_a, g_mix_b, g_mix_c, g_patch, g_in, g_bias, g_out,
    wide_in, wide_out, square, copy_sem, out_sem,
):
    chans, chunks = plan.chans, plan.chunks
    moves = []
    for place, (source, target) in enumerate(zip((ia, ib, ic, ja, jb, jc), (oa, ob, oc, ga, gb, gc))):
        moves.append(pltpu.make_async_copy(source, target, copy_sem.at[place]))
    g_patch[...] = jnp.zeros_like(g_patch)
    for layer in reversed(range(LAYERS)):
        if layer == 0:
            for move in moves[:6]:
                move.start()
        first = (LAYERS - 1 - layer) * plan.steps
        for step in range(chunks):
            lanes = pl.ds(step * CHUNK, CHUNK)
            for part in range(CHUNK // LANES):
                spot = pl.ds(step * CHUNK + part * LANES, LANES)
                wide_in[layer, :, spot] = held[first + step, pl.ds(part * chans, chans), :].astype(f32)
            for part in range(chans // LANES):
                spot = pl.ds(part * LANES, LANES)
                wide_out[layer, lanes, spot] = held[first + step, pl.ds(plan.half + part * CHUNK, CHUNK), :].astype(f32)
            for place, (source, target) in enumerate(
                ((wide_in.at[layer, :, lanes], g_in.at[layer, :, lanes]), (wide_out.at[layer, lanes], g_out.at[layer, lanes]))
            ):
                moves.append(pltpu.make_async_copy(source, target, out_sem.at[layer, step, place]))
                moves[-1].start()
        offset = 0
        for kind, target in enumerate((g_mix_a, g_mix_b, g_mix_c)):
            width, rows_k, size = plan.widths[kind], plan.padded[kind], plan.wide[kind]
            for part in range(size // LANES):
                place = plan.places[kind] + part * rows_k
                square[0:rows_k, part * LANES : (part + 1) * LANES] = held[first + chunks, pl.ds(place, rows_k), :].astype(
                    f32
                )
            whole = square[0:rows_k, 0:size]
            target[:, layer, :] = whole[0:width, 0:width]
            row = lax.broadcasted_iota(jnp.int32, (rows_k, size), 0)
            col = lax.broadcasted_iota(jnp.int32, (rows_k, size), 1)
            column = jnp.sum(jnp.where(col == width, whole, 0.0), axis=1, keepdims=True)
            turned = jnp.sum(jnp.where((row == col) & (row < width), column, 0.0), axis=0, keepdims=True)
            g_patch[layer : layer + 1, offset : offset + width] = turned[:, 0:width]
            offset += width
        small = square[width : width + 7 + plan.hid // chans, :]
        for place, row in enumerate((0, 2, 3, 5)):
            g_scales[layer, place : place + 1, :] = small[row : row + 1]
        for place, row in enumerate((1, 4, 6)):
            g_shifts[place, layer : layer + 1, :] = small[row : row + 1]
        for place in range(plan.hid // chans):
            g_bias[layer : layer + 1, place * chans : (place + 1) * chans] = small[7 + place : 8 + place]
    for move in moves:
        move.wait()


def solution(mesh):
    sections, dp = mesh.shape["section"], mesh.shape["dp"]

    def run(*args):
        images, weight_in = args[:3], args[13]
        slots = images[0].shape[0] // (sections * dp)
        widths = tuple(image.shape[1] for image in images)
        plan = Plan(sections, dp, slots, widths, weight_in.shape[1], weight_in.shape[2])
        split_in = P("dp", None, None)
        split_out = P(("dp", "section"), None, None)
        in_specs = (split_in,) * 6 + (P("dp", None),) + (P(),) * 9
        out_specs = (split_out,) * 6 + (P(),) * 9
        whole = jax.shard_map(
            functools.partial(body, plan), mesh=mesh, in_specs=in_specs, out_specs=out_specs, check_vma=False
        )
        return whole(*args)

    return run
```

```python
import functools

import jax
import jax.numpy as jnp
from jax import lax
from jax.experimental import pallas as pl
from jax.experimental.pallas import tpu as pltpu
from jax.sharding import PartitionSpec as P

MESH = pl.DeviceIdType.MESH
f32 = jnp.float32
bf16 = jnp.bfloat16
LAYERS = 2
KINDS = 3
LANES = 128
ROWS = 16
CHUNK = 256
SLACK = 2
BLOCK = 32
HALF_LOG2E = -0.7213475204444817
HALF_ROOT = 0.7071067811865476
PDF_SCALE = 0.3989422804014327


def up(value, unit):
    return -(-value // unit) * unit


def nt(left, right):
    return lax.dot_general(left, right, (((1,), (1,)), ((), ())), preferred_element_type=f32)


def nn(left, right):
    return jnp.dot(left, right, preferred_element_type=f32)


def col_sum(value):
    return jnp.sum(value, axis=0, keepdims=True)


def cuts(total, pieces):
    tiles = total // ROWS
    marks = [tiles * k // pieces * ROWS for k in range(pieces + 1)]
    return [(marks[k], marks[k + 1] - marks[k]) for k in range(pieces)]


class Plan:
    def __init__(self, sections, dp, slots, widths, chans, hid):
        self.sections, self.dp, self.slots, self.widths, self.chans, self.hid = sections, dp, slots, widths, chans, hid
        self.padded = tuple(up(width + 1, ROWS) for width in widths)
        self.wide = tuple(up(rows, LANES) for rows in self.padded)
        self.segments = []
        start = 0
        for kind in range(KINDS):
            for slot in range(slots):
                self.segments.append((kind, slot, start))
                start += self.padded[kind]
        self.rows = start
        self.chunks = hid // CHUNK
        self.steps = self.chunks + 1
        self.pieces = LAYERS * self.steps
        self.depth = min(4, dp // 2)
        self.outer = dp // (2 * self.depth)
        self.size = 2 * chans * CHUNK // LANES
        self.half, self.quarter, self.eighth = self.size // 2, self.size // 4, self.size // 8
        self.last = self.eighth // self.depth
        self.places, place = {}, 0
        for kind in reversed(range(KINDS)):
            self.places[kind] = place
            place += self.padded[kind] * (self.wide[kind] // LANES)
        assert place <= self.size and self.last % ROWS == 0 and sections == 4 and self.depth > 1


def kernel(
    plan,
    xa, xb, xc, ca, cb, cc, counts, scales, shifts, mix_a, mix_b, mix_c, patch_bias, bias_in, w_in_hbm, w_out_hbm,
    oa, ob, oc, ga, gb, gc, result,
    w_in, w_out, pad, pbias, aff, bias32, mat_a, mat_b, mat_c, tam_a, tam_b, tam_c,
    xs, x1s, us, hs, ds, z2, acc, grad, dvr, dvt, z2t, da, vecs, bgrad,
    own, land0, land1, land2, land3,
    io_sem, send_sem, recv_sem,
):
    widths, padded, wide = plan.widths, plan.padded, plan.wide
    slots, chans, rows = plan.slots, plan.chans, plan.rows
    section = lax.axis_index("section")
    dp = lax.axis_index("dp")
    core = lax.rem(dp, 2)
    deep = lax.rem(lax.div(dp, 2), plan.depth)
    block = dp - lax.rem(dp, 2 * plan.depth)
    bit0, bit1 = lax.rem(section, 2), lax.div(section, 2)
    first = jnp.where(core == 0, bit0, bit1)
    second = jnp.where(core == 0, bit1, bit0)
    flip0 = section + 1 - 2 * bit0
    flip1 = section + 2 - 4 * bit1
    first_to = (jnp.where(core == 0, flip0, flip1), dp)
    second_to = (jnp.where(core == 0, flip1, flip0), dp)
    core_to = (section, dp + 1 - 2 * core)

    def deep_to(step):
        return (section, block + lax.rem(deep + step, plan.depth) * 2 + core)

    partners = [core_to, first_to, second_to] + [deep_to(step) for step in range(1, plan.depth)]
    barrier = pltpu.get_barrier_semaphore()
    for partner in partners:
        pl.semaphore_signal(barrier, inc=1, device_id=partner, device_id_type=MESH)

    raw_x, raw_c = (oa, ob, oc), (ga, gb, gc)
    fetches = []
    mine = pl.ds(pl.multiple_of(section * slots, slots), slots)
    pairs = list(zip((xa, xb, xc), raw_x)) + list(zip((ca, cb, cc), raw_c))
    for place, (source, target) in enumerate(pairs):
        fetches.append(pltpu.make_async_copy(source.at[:, mine, :], target, io_sem.at[place]))
    fetches.append(pltpu.make_async_copy(w_in_hbm, w_in, io_sem.at[6]))
    fetches.append(pltpu.make_async_copy(w_out_hbm, w_out, io_sem.at[7]))
    for fetch in fetches[:3] + fetches[6:] + fetches[3:6]:
        fetch.start()

    for layer in range(LAYERS):
        aff[layer, 0:4, :] = scales[layer].astype(f32)
        aff[layer, 4:7, :] = shifts[:, layer, :].astype(f32)
        bias32[layer, :, :] = bias_in[...].astype(f32)[layer : layer + 1]
    pbias[...] = jnp.zeros_like(pbias)
    pbias[0:LAYERS, 0 : patch_bias.shape[1]] = patch_bias[...].astype(f32)
    pad[...] = jnp.zeros_like(pad)

    mats, tams = (mat_a, mat_b, mat_c), (tam_a, tam_b, tam_c)
    offset = 0
    for kind, source in enumerate((mix_a, mix_b, mix_c)):
        width, rows_k, size = widths[kind], padded[kind], wide[kind]
        turned = pltpu.roll(pbias[...], pbias.shape[1] - offset, 1) if offset else pbias[...]
        offset += width
        row = lax.broadcasted_iota(jnp.int32, (size, size), 0)
        col = lax.broadcasted_iota(jnp.int32, (size, size), 1)
        for layer in range(LAYERS):
            pad[0:size, 0:size] = jnp.zeros((size, size), f32)
            pad[0:width, 0:width] = source[:, layer, :].astype(f32)
            biases = turned[layer : layer + 1, 0:size]
            column = jnp.sum(jnp.where(row == col, biases, 0.0), axis=1, keepdims=True)
            whole = jnp.where((col == width) & (row < width), column, pad[0:size, 0:size])
            mats[kind][layer] = whole[0:rows_k, 0:rows_k].astype(bf16)
            tams[kind][layer] = whole.T[0:rows_k, 0:rows_k].astype(bf16)

    def padded_image(value, kind):
        width, rows_k = widths[kind], padded[kind]
        edge = width // 8 * 8
        pad[edge:rows_k, :] = jnp.zeros((rows_k - edge, chans), f32)
        pad[0:width, :] = value
        return pad[0:rows_k, :]

    def live(kind, slot):
        return (slot < counts[section, kind]).astype(f32)

    for kind, slot, start in plan.segments:
        if slot == 0:
            fetches[kind].wait()
        xs[0, pl.ds(start, padded[kind]), :] = padded_image(raw_x[kind][:, slot, :].astype(f32), kind).astype(bf16)

    def blocks(kind):
        return [(low, min(BLOCK, padded[kind] - low)) for low in range(0, padded[kind], BLOCK)]

    def rows_from(low, shape):
        return lax.broadcasted_iota(jnp.int32, shape, 0) + low

    def mixer_input(kind, low, x, vec):
        z = vec[0:1] * x + vec[4:5]
        if low <= widths[kind] < low + x.shape[0]:
            z = jnp.where(rows_from(low, z.shape) == widths[kind], 1.0, z)
        return z.astype(bf16)

    def fold(value):
        return value.reshape(-1, 8, chans).sum(axis=0)

    def forward(layer):
        vec = aff[layer]
        for kind, slot, start in plan.segments:
            span = pl.ds(start, padded[kind])
            for low, size in blocks(kind):
                part = pl.ds(start + low, size)
                z2[part, :] = mixer_input(kind, low, xs[layer, part, :].astype(f32), vec)
            product = nn(mats[kind][layer], z2[span, :])
            for low, size in blocks(kind):
                part = pl.ds(start + low, size)
                p = product[low : low + size]
                us[layer, part, :] = p.astype(bf16)
                x1 = (xs[layer, part, :].astype(f32) + vec[1:2] * p).astype(bf16)
                x1s[layer, part, :] = x1
                z2[part, :] = (vec[2:3] * x1.astype(f32) + vec[5:6]).astype(bf16)
                if layer < LAYERS - 1:
                    acc[part, :] = jnp.broadcast_to(vec[6:7], (size, chans))

        if layer == 0:
            fetches[6].wait()
            fetches[7].wait()

        for chunk in range(plan.chunks):
            lanes = pl.ds(chunk * CHUNK, CHUNK)
            bias = bias32[layer, :, lanes]
            first_weight = w_in[layer, :, lanes]
            second_weight = w_out[layer, lanes, :]
            for start, size in cuts(rows, 4):
                span = pl.ds(start, size)
                product = nn(z2[span, :], first_weight)
                for low in range(0, size, BLOCK):
                    high = min(low + BLOCK, size)
                    a = product[low:high] + bias
                    cdf = 0.5 + 0.5 * lax.erf(a * HALF_ROOT)
                    slope = a * jnp.exp2(a * a * HALF_LOG2E) * PDF_SCALE
                    block_span = pl.ds(start + low, high - low)
                    hs[layer, chunk, block_span, :] = (a * cdf).astype(bf16)
                    ds[layer, chunk, block_span, :] = (cdf + slope).astype(bf16)
                if layer < LAYERS - 1:
                    acc[span, :] += nn(hs[layer, chunk, span, :], second_weight)

        if layer < LAYERS - 1:
            for kind, slot, start in plan.segments:
                span = pl.ds(start, padded[kind])
                xs[layer + 1, span, :] = (x1s[layer, span, :].astype(f32) + vec[3:4] * acc[span, :]).astype(bf16)

    for layer in range(LAYERS):
        forward(layer)

    for kind, slot, start in plan.segments:
        if slot == 0:
            fetches[KINDS + kind].wait()
        cot = raw_c[kind][:, slot, :].astype(f32) * live(kind, slot)
        grad[pl.ds(start, padded[kind]), :] = padded_image(cot, kind).astype(bf16)

    pl.semaphore_wait(barrier, len(partners))

    base0 = core * plan.half
    base1 = base0 + first * plan.quarter
    base2 = base1 + second * plan.eighth
    base3 = base2 + deep * plan.last

    def at(ref, piece, start, size):
        return ref.at[piece, pl.ds(pl.multiple_of(start, ROWS), size)]

    def send(piece, hop, source, target, to):
        return pltpu.make_async_remote_copy(
            src_ref=source,
            dst_ref=target,
            send_sem=send_sem.at[hop],
            recv_sem=recv_sem.at[piece, hop],
            device_id=to,
            device_id_type=MESH,
        )

    def hop0(piece):
        return [send(piece, 0, at(own, piece, (1 - core) * plan.half, plan.half), land0.at[piece], core_to)]

    def hop1(piece):
        return [send(piece, 1, at(land0, piece, (1 - first) * plan.quarter, plan.quarter), land1.at[piece], first_to)]

    def hop2(piece):
        return [send(piece, 2, at(land1, piece, (1 - second) * plan.eighth, plan.eighth), land2.at[piece], second_to)]

    def hop3(piece):
        return [
            send(
                piece,
                3,
                at(land2, piece, lax.rem(deep + step, plan.depth) * plan.last, plan.last),
                land3.at[piece, step - 1],
                deep_to(step),
            )
            for step in range(1, plan.depth)
        ]

    def hop4(piece):
        spot = at(result, piece, base3, plan.last)
        return [send(piece, 4, spot, spot, deep_to(step)) for step in range(1, plan.depth)]

    def hop5(piece):
        spot = at(result, piece, base2, plan.eighth)
        return [send(piece, 5, spot, spot, second_to)]

    def hop6(piece):
        spot = at(result, piece, base1, plan.quarter)
        return [send(piece, 6, spot, spot, first_to)]

    def hop7(piece):
        spot = at(result, piece, base0, plan.half)
        return [send(piece, 7, spot, spot, core_to)]

    others = plan.last * (plan.depth - 1)

    def brought(piece, hop):
        whole = [
            land0.at[piece],
            land1.at[piece],
            land2.at[piece],
            land3.at[piece],
            at(result, piece, base2, others),
            at(result, piece, base2, plan.eighth),
            at(result, piece, base1, plan.quarter),
            at(result, piece, base0, plan.half),
        ][hop]
        return send(piece, hop, whole, whole, core_to)

    totals = [land0, land1, land2, land3, land3, land2, land1, land0]

    def start(copies):
        for copy in copies:
            copy.start()

    def get(ref, piece, start, size):
        return ref[piece, pl.ds(pl.multiple_of(start, ROWS), size), :].astype(f32)

    def add0(piece):
        land0[piece] = (land0[piece].astype(f32) + get(own, piece, base0, plan.half)).astype(bf16)

    def add1(piece):
        land1[piece] = (land1[piece].astype(f32) + get(land0, piece, first * plan.quarter, plan.quarter)).astype(bf16)

    def add2(piece):
        land2[piece] = (land2[piece].astype(f32) + get(land1, piece, second * plan.eighth, plan.eighth)).astype(bf16)

    def add3(piece):
        total = get(land2, piece, deep * plan.last, plan.last)
        for step in range(plan.depth - 1):
            total = total + land3[piece, step].astype(f32)
        result[piece, pl.ds(pl.multiple_of(base3, ROWS), plan.last), :] = total.astype(bf16)

    def nothing(piece):
        pass

    hops = [hop0, hop1, hop2, hop3, hop4, hop5, hop6, hop7]
    adds = [add0, add1, add2, add3, nothing, nothing, nothing, nothing]

    def tick(moment):
        for stage in range(len(hops) + 1):
            piece = moment - SLACK * stage

            @pl.when((piece >= 0) & (piece < plan.pieces))
            def _(stage=stage, piece=piece):
                if stage > 0:
                    brought(piece, stage - 1).wait_recv()
                    adds[stage - 1](piece)
                if stage < len(hops):
                    start(hops[stage](piece))

    def backward(turn):
        layer = LAYERS - 1 - turn
        vec = aff[layer]
        bias_sum = jnp.zeros((1, chans), f32)
        vecs[...] = jnp.zeros_like(vecs)
        for start in range(0, rows, LANES):
            span = pl.ds(start, min(LANES, rows - start))
            g = grad[span, :].astype(f32)
            dv = vec[3:4] * g
            bias_sum = bias_sum + col_sum(dv)
            low = dv.astype(bf16)
            dvr[span, :] = low
            dvt[:, span] = low.T
            z2t[:, span] = (vec[2:3] * x1s[layer, span, :].astype(f32) + vec[5:6]).astype(bf16).T
            acc[span, :] = jnp.zeros((span.size, chans), f32)

        def step(chunk, carry):
            lanes = pl.ds(pl.multiple_of(chunk * CHUNK, CHUNK), CHUNK)
            first_weight = w_in[layer, :, lanes]
            second_weight = w_out[layer, lanes, :]
            total = jnp.zeros((8, CHUNK), f32)
            for start, size in cuts(rows, 4):
                span = pl.ds(start, size)
                dh = nt(dvr[span, :], second_weight)
                for low in range(0, size, BLOCK):
                    high = min(low + BLOCK, size)
                    block_span = pl.ds(start + low, high - low)
                    dact = dh[low:high] * ds[layer, chunk, block_span, :].astype(f32)
                    total = total + dact.reshape(-1, 8, CHUNK).sum(axis=0)
                    da[block_span, :] = dact.astype(bf16)
                acc[span, :] += nt(da[span, :], first_weight)
            bgrad[:, lanes] = col_sum(total)
            piece = turn * plan.steps + chunk
            gin = nn(z2t[...], da[...]).astype(bf16)
            for part in range(CHUNK // LANES):
                own[piece, pl.ds(part * chans, chans), :] = gin[:, part * LANES : (part + 1) * LANES]
            gout = nn(dvt[...], hs[layer, chunk]).astype(bf16).T
            vecs[...] += (gout.astype(f32) * second_weight.astype(f32)).reshape(-1, 8, chans).sum(axis=0)
            for part in range(chans // LANES):
                own[piece, pl.ds(plan.half + part * CHUNK, CHUNK), :] = gout[:, part * LANES : (part + 1) * LANES]
            tick(piece)
            return carry

        lax.fori_loop(0, plan.chunks, step, 0)

        piece = turn * plan.steps + plan.chunks
        sums = [jnp.zeros((8, chans), f32) for _ in range(5)]
        for kind in range(KINDS):
            width, rows_k, size = widths[kind], padded[kind], wide[kind]
            mix_grad = jnp.zeros((rows_k, rows_k), f32)
            for seg_kind, slot, start in plan.segments:
                if seg_kind != kind:
                    continue
                span = pl.ds(start, rows_k)
                for low, count in blocks(kind):
                    part = pl.ds(start + low, count)
                    dz2 = acc[part, :]
                    sums[3] = sums[3] + fold(x1s[layer, part, :].astype(f32) * dz2)
                    sums[4] = sums[4] + fold(dz2)
                    low_g = (grad[part, :].astype(f32) + vec[2:3] * dz2).astype(bf16)
                    grad[part, :] = low_g
                    g1 = low_g.astype(f32)
                    sums[2] = sums[2] + fold(g1 * us[layer, part, :].astype(f32))
                    dvr[part, :] = (vec[1:2] * g1).astype(bf16)
                    z2[part, :] = mixer_input(kind, low, xs[layer, part, :].astype(f32), vec)
                mix_grad = mix_grad + nt(dvr[span, :], z2[span, :])
                product = nn(tams[kind][layer], dvr[span, :])
                for low, count in blocks(kind):
                    part = pl.ds(start + low, count)
                    dz = product[low : low + count]
                    if low + count > width:
                        dz = jnp.where(rows_from(low, dz.shape) < width, dz, 0.0)
                    sums[0] = sums[0] + fold(xs[layer, part, :].astype(f32) * dz)
                    sums[1] = sums[1] + fold(dz)
                    grad[part, :] = (grad[part, :].astype(f32) + vec[0:1] * dz).astype(bf16)
            pad[0:rows_k, 0:rows_k] = mix_grad
            if kind == KINDS - 1:
                for place in range(5):
                    pad[width + place : width + place + 1, :] = col_sum(sums[place])
                pad[width + 5 : width + 6, :] = (col_sum(vecs[...]) + vec[6:7] * bias_sum) / vec[3:4]
                pad[width + 6 : width + 7, :] = bias_sum
                for place in range(plan.hid // chans):
                    spot = width + 7 + place
                    pad[spot : spot + 1, :] = bgrad[:, place * chans : (place + 1) * chans]
            for part in range(size // LANES):
                place = plan.places[kind] + part * rows_k
                own[piece, pl.ds(place, rows_k), :] = pad[0:rows_k, part * LANES : (part + 1) * LANES].astype(bf16)
        tick(piece)

    for turn in range(LAYERS):
        backward(turn)

    def shown(buffer, kind, slot, start):
        return buffer[pl.ds(start, padded[kind]), :].astype(f32)[0 : widths[kind]]

    acc[...] = jnp.zeros_like(acc)

    def drain(moment, carry):
        tick(moment)

        @pl.when(moment == plan.pieces)
        def _():
            for kind, slot, begin in plan.segments:
                raw_c[kind][:, slot, :] = shown(grad, kind, slot, begin).astype(bf16)

        @pl.when(moment < plan.pieces + plan.chunks)
        def _():
            chunk = moment - plan.pieces
            lanes = pl.ds(pl.multiple_of(chunk * CHUNK, CHUNK), CHUNK)
            acc[...] += nn(hs[LAYERS - 1, chunk], w_out[LAYERS - 1, lanes, :])

        @pl.when(moment == plan.pieces + plan.chunks)
        def _():
            vec = aff[LAYERS - 1]
            for kind, slot, begin in plan.segments:
                span = pl.ds(begin, padded[kind])
                y = (x1s[LAYERS - 1, span, :].astype(f32) + vec[3:4] * (acc[span, :] + vec[6:7])).astype(bf16)
                raw_x[kind][:, slot, :] = (y.astype(f32) * live(kind, slot)).astype(bf16)[0 : widths[kind]]

        return carry

    lax.fori_loop(plan.pieces, plan.pieces + SLACK * len(hops), drain, 0)

    for hop, total in enumerate(totals):
        pltpu.make_async_remote_copy(
            src_ref=total,
            dst_ref=total,
            send_sem=send_sem.at[hop],
            recv_sem=recv_sem.at[0, hop],
            device_id=core_to,
            device_id_type=MESH,
        ).wait_send()


def body(plan, *args):
    slots, chans, hid, rows = plan.slots, plan.chans, plan.hid, plan.rows
    images = [(width, slots, chans) for width in plan.widths]
    anywhere = pl.BlockSpec(memory_space=pl.ANY)
    vmem = pl.BlockSpec(memory_space=pltpu.VMEM)
    in_specs = [anywhere] * 6 + [pl.BlockSpec(memory_space=pltpu.SMEM)] + [vmem] * 7 + [anywhere] * 2
    (
        *pictures,
        live_counts,
        scales,
        shifts,
        mix_a,
        mix_b,
        mix_c,
        patch_bias,
        weight_in,
        bias_in,
        weight_out,
    ) = args
    scratch = [
        pltpu.VMEM((LAYERS, chans, hid), bf16),
        pltpu.VMEM((LAYERS, hid, chans), bf16),
        pltpu.VMEM((max(plan.wide), chans), f32),
        pltpu.VMEM((8, up(patch_bias.shape[1], LANES)), f32),
        pltpu.VMEM((LAYERS, 8, chans), f32),
        pltpu.VMEM((LAYERS, 1, hid), f32),
    ]
    scratch += [pltpu.VMEM((LAYERS, size, size), bf16) for size in plan.padded * 2]
    scratch += [
        pltpu.VMEM((LAYERS, rows, chans), bf16),
        pltpu.VMEM((LAYERS, rows, chans), bf16),
        pltpu.VMEM((LAYERS, rows, chans), bf16),
        pltpu.VMEM((LAYERS, plan.chunks, rows, CHUNK), bf16),
        pltpu.VMEM((LAYERS, plan.chunks, rows, CHUNK), bf16),
        pltpu.VMEM((rows, chans), bf16),
        pltpu.VMEM((rows, chans), f32),
        pltpu.VMEM((rows, chans), bf16),
        pltpu.VMEM((rows, chans), bf16),
        pltpu.VMEM((chans, rows), bf16),
        pltpu.VMEM((chans, rows), bf16),
        pltpu.VMEM((rows, CHUNK), bf16),
        pltpu.VMEM((8, chans), f32),
        pltpu.VMEM((1, hid), f32),
        pltpu.VMEM((plan.pieces, plan.size, LANES), bf16),
        pltpu.VMEM((plan.pieces, plan.half, LANES), bf16),
        pltpu.VMEM((plan.pieces, plan.quarter, LANES), bf16),
        pltpu.VMEM((plan.pieces, plan.eighth, LANES), bf16),
        pltpu.VMEM((plan.pieces, plan.depth - 1, plan.last, LANES), bf16),
        pltpu.SemaphoreType.DMA((8,)),
        pltpu.SemaphoreType.DMA((8,)),
        pltpu.SemaphoreType.DMA((plan.pieces, 8)),
    ]
    out_shape = [pltpu.VMEM(shape, bf16) for shape in images * 2]
    stays = pltpu.VMEM if plan.outer == 1 else jax.ShapeDtypeStruct
    out_shape.append(stays((plan.pieces, plan.size, LANES), bf16))
    views = [picture.transpose(1, 0, 2) for picture in pictures]
    mixes = [mix.transpose(1, 0, 2) for mix in (mix_a, mix_b, mix_c)]
    *shown, sums = pl.pallas_call(
        functools.partial(kernel, plan),
        out_shape=out_shape,
        in_specs=in_specs,
        out_specs=[vmem] * 7,
        scratch_shapes=scratch,
        compiler_params=pltpu.CompilerParams(
            collective_id=0, has_side_effects=True, vmem_limit_bytes=(55 if plan.outer == 1 else 60) * 1024 * 1024
        ),
    )(*views, live_counts, scales, shifts.transpose(1, 0, 2), *mixes, patch_bias, bias_in, weight_in, weight_out)
    if plan.outer > 1:
        ring = 2 * plan.depth
        groups = [[low + ring * high for high in range(plan.outer)] for low in range(ring)]
        sums = lax.psum(sums, "dp", axis_index_groups=groups)
    finals = [jax.ShapeDtypeStruct(shape, bf16) for shape in images * 2]
    finals += [
        jax.ShapeDtypeStruct(shape, f32)
        for shape in [(LAYERS, 4, chans), (3, LAYERS, chans)]
        + [(width, LAYERS, width) for width in plan.widths]
        + [(LAYERS, sum(plan.widths)), (LAYERS, chans, hid), (LAYERS, hid), (LAYERS, hid, chans)]
    ]
    out = pl.pallas_call(
        functools.partial(unpack, plan),
        out_shape=finals,
        in_specs=[vmem] * 7,
        out_specs=[anywhere] * 6 + [vmem] * 2 + [anywhere] * 3 + [vmem, anywhere, vmem, anywhere],
        scratch_shapes=[
            pltpu.VMEM((LAYERS, chans, hid), f32),
            pltpu.VMEM((LAYERS, hid, chans), f32),
            pltpu.VMEM((LAYERS, max(plan.wide), chans), f32),
            *(pltpu.VMEM((width, LAYERS, width), f32) for width in plan.widths),
            pltpu.SemaphoreType.DMA((6,)),
            pltpu.SemaphoreType.DMA((KINDS,)),
            pltpu.SemaphoreType.DMA((LAYERS, plan.chunks, 2)),
        ],
        compiler_params=pltpu.CompilerParams(vmem_limit_bytes=24 * 1024 * 1024),
    )(*shown, sums)
    order = [value.transpose(1, 0, 2) for value in out[:6]]
    return (*order, out[6], out[7].transpose(1, 0, 2), *(mix.transpose(1, 0, 2) for mix in out[8:11]), *out[11:])


def unpack(
    plan, ia, ib, ic, ja, jb, jc, held,
    oa, ob, oc, ga, gb, gc, g_scales, g_shifts, g_mix_a, g_mix_b, g_mix_c, g_patch, g_in, g_bias, g_out,
    wide_in, wide_out, square, mix_a, mix_b, mix_c, copy_sem, mix_sem, out_sem,
):
    chans, chunks = plan.chans, plan.chunks
    moves = []
    for place, (source, target) in enumerate(zip((ia, ib, ic, ja, jb, jc), (oa, ob, oc, ga, gb, gc))):
        moves.append(pltpu.make_async_copy(source, target, copy_sem.at[place]))
    for move in moves:
        move.start()
    g_patch[...] = jnp.zeros_like(g_patch)
    firsts = [(LAYERS - 1 - layer) * plan.steps for layer in range(LAYERS)]
    offset = 0
    for kind, (stage, target) in enumerate(zip((mix_a, mix_b, mix_c), (g_mix_a, g_mix_b, g_mix_c))):
        width, rows_k, size = plan.widths[kind], plan.padded[kind], plan.wide[kind]
        for layer in range(LAYERS):
            for part in range(size // LANES):
                spot = pl.ds(plan.places[kind] + part * rows_k, rows_k)
                value = held[firsts[layer] + chunks, spot, :].astype(f32)
                square[layer, 0:rows_k, part * LANES : (part + 1) * LANES] = value
            whole = square[layer, 0:rows_k, 0:size]
            stage[:, layer, :] = whole[0:width, 0:width]
            row = lax.broadcasted_iota(jnp.int32, (rows_k, size), 0)
            col = lax.broadcasted_iota(jnp.int32, (rows_k, size), 1)
            column = jnp.sum(jnp.where(col == width, whole, 0.0), axis=1, keepdims=True)
            turned = jnp.sum(jnp.where((row == col) & (row < width), column, 0.0), axis=0, keepdims=True)
            g_patch[layer : layer + 1, offset : offset + width] = turned[:, 0:width]
        moves.append(pltpu.make_async_copy(stage, target, mix_sem.at[kind]))
        moves[-1].start()
        offset += width
    for layer in reversed(range(LAYERS)):
        for step in range(chunks):
            lanes = pl.ds(step * CHUNK, CHUNK)
            piece = firsts[layer] + step
            for part in range(CHUNK // LANES):
                spot = pl.ds(step * CHUNK + part * LANES, LANES)
                wide_in[layer, :, spot] = held[piece, pl.ds(part * chans, chans), :].astype(f32)
            for part in range(chans // LANES):
                spot = pl.ds(part * LANES, LANES)
                wide_out[layer, lanes, spot] = held[piece, pl.ds(plan.half + part * CHUNK, CHUNK), :].astype(f32)
            for place, (source, target) in enumerate(
                ((wide_in.at[layer, :, lanes], g_in.at[layer, :, lanes]), (wide_out.at[layer, lanes], g_out.at[layer, lanes]))
            ):
                moves.append(pltpu.make_async_copy(source, target, out_sem.at[layer, step, place]))
                moves[-1].start()
        width = plan.widths[KINDS - 1]
        small = square[layer, width : width + 7 + plan.hid // chans, :]
        for place, row in enumerate((0, 2, 3, 5)):
            g_scales[layer, place : place + 1, :] = small[row : row + 1]
        for place, row in enumerate((1, 4, 6)):
            g_shifts[place, layer : layer + 1, :] = small[row : row + 1]
        for place in range(plan.hid // chans):
            g_bias[layer : layer + 1, place * chans : (place + 1) * chans] = small[7 + place : 8 + place]
    for move in moves:
        move.wait()


def solution(mesh):
    sections, dp = mesh.shape["section"], mesh.shape["dp"]

    def run(*args):
        images, weight_in = args[:3], args[13]
        slots = images[0].shape[0] // (sections * dp)
        widths = tuple(image.shape[1] for image in images)
        plan = Plan(sections, dp, slots, widths, weight_in.shape[1], weight_in.shape[2])
        split_in = P("dp", None, None)
        split_out = P(("dp", "section"), None, None)
        in_specs = (split_in,) * 6 + (P("dp", None),) + (P(),) * 9
        out_specs = (split_out,) * 6 + (P(),) * 9
        whole = jax.shard_map(
            functools.partial(body, plan), mesh=mesh, in_specs=in_specs, out_specs=out_specs, check_vma=False
        )
        return whole(*args)

    return run
```

```python
import functools

import jax
import jax.numpy as jnp
from jax import lax
from jax.experimental import pallas as pl
from jax.experimental.pallas import tpu as pltpu
from jax.sharding import PartitionSpec as P

MESH = pl.DeviceIdType.MESH
f32 = jnp.float32
bf16 = jnp.bfloat16
LAYERS = 2
KINDS = 3
LANES = 128
ROWS = 16
CHUNK = 256
SLACK = 2
BLOCK = 32
HALF_LOG2E = -0.7213475204444817
HALF_ROOT = 0.7071067811865476
PDF_SCALE = 0.3989422804014327


def up(value, unit):
    return -(-value // unit) * unit


def nt(left, right):
    return lax.dot_general(left, right, (((1,), (1,)), ((), ())), preferred_element_type=f32)


def nn(left, right):
    return jnp.dot(left, right, preferred_element_type=f32)


def col_sum(value):
    return jnp.sum(value, axis=0, keepdims=True)


def cuts(total, pieces):
    tiles = total // ROWS
    marks = [tiles * k // pieces * ROWS for k in range(pieces + 1)]
    return [(marks[k], marks[k + 1] - marks[k]) for k in range(pieces)]


class Plan:
    def __init__(self, sections, dp, slots, widths, chans, hid):
        self.sections, self.dp, self.slots, self.widths, self.chans, self.hid = sections, dp, slots, widths, chans, hid
        self.padded = tuple(up(width + 1, ROWS) for width in widths)
        self.wide = tuple(up(rows, LANES) for rows in self.padded)
        self.segments = []
        start = 0
        for kind in range(KINDS):
            for slot in range(slots):
                self.segments.append((kind, slot, start))
                start += self.padded[kind]
        self.rows = start
        self.chunks = hid // CHUNK
        self.steps = self.chunks + 1
        self.pieces = LAYERS * self.steps
        self.depth = min(4, dp // 2)
        self.outer = dp // (2 * self.depth)
        self.size = 2 * chans * CHUNK // LANES
        self.half, self.quarter, self.eighth = self.size // 2, self.size // 4, self.size // 8
        self.last = self.eighth // self.depth
        self.places, place = {}, 0
        for kind in reversed(range(KINDS)):
            self.places[kind] = place
            place += self.padded[kind] * (self.wide[kind] // LANES)
        assert place <= self.size and self.last % ROWS == 0 and sections == 4 and self.depth > 1


def kernel(
    plan,
    xa, xb, xc, ca, cb, cc, counts, scales, shifts, mix_a, mix_b, mix_c, patch_bias, bias_in, w_in_hbm, w_out_hbm,
    oa, ob, oc, ga, gb, gc, result,
    w_in, w_out, pad, pbias, aff, bias32, mat_a, mat_b, mat_c, tam_a, tam_b, tam_c,
    xs, x1s, us, hs, ds, z2, acc, grad, dvr, dvt, z2t, da, vecs, bgrad,
    own, land0, land1, land2, land3,
    io_sem, send_sem, recv_sem,
):
    widths, padded, wide = plan.widths, plan.padded, plan.wide
    slots, chans, rows = plan.slots, plan.chans, plan.rows
    section = lax.axis_index("section")
    dp = lax.axis_index("dp")
    core = lax.rem(dp, 2)
    deep = lax.rem(lax.div(dp, 2), plan.depth)
    block = dp - lax.rem(dp, 2 * plan.depth)
    bit0, bit1 = lax.rem(section, 2), lax.div(section, 2)
    first = jnp.where(core == 0, bit0, bit1)
    second = jnp.where(core == 0, bit1, bit0)
    flip0 = section + 1 - 2 * bit0
    flip1 = section + 2 - 4 * bit1
    first_to = (jnp.where(core == 0, flip0, flip1), dp)
    second_to = (jnp.where(core == 0, flip1, flip0), dp)
    core_to = (section, dp + 1 - 2 * core)

    def deep_to(step):
        return (section, block + lax.rem(deep + step, plan.depth) * 2 + core)

    partners = [core_to, first_to, second_to] + [deep_to(step) for step in range(1, plan.depth)]
    barrier = pltpu.get_barrier_semaphore()
    for partner in partners:
        pl.semaphore_signal(barrier, inc=1, device_id=partner, device_id_type=MESH)

    raw_x, raw_c = (oa, ob, oc), (ga, gb, gc)
    fetches = []
    mine = pl.ds(pl.multiple_of(section * slots, slots), slots)
    pairs = list(zip((xa, xb, xc), raw_x)) + list(zip((ca, cb, cc), raw_c))
    for place, (source, target) in enumerate(pairs):
        fetches.append(pltpu.make_async_copy(source.at[:, mine, :], target, io_sem.at[place]))
    fetches.append(pltpu.make_async_copy(w_in_hbm, w_in, io_sem.at[6]))
    fetches.append(pltpu.make_async_copy(w_out_hbm, w_out, io_sem.at[7]))
    for fetch in fetches[:3] + fetches[6:] + fetches[3:6]:
        fetch.start()

    for layer in range(LAYERS):
        aff[layer, 0:4, :] = scales[layer].astype(f32)
        aff[layer, 4:7, :] = shifts[:, layer, :].astype(f32)
        bias32[layer, :, :] = bias_in[...].astype(f32)[layer : layer + 1]
    pbias[...] = jnp.zeros_like(pbias)
    pbias[0:LAYERS, 0 : patch_bias.shape[1]] = patch_bias[...].astype(f32)
    pad[...] = jnp.zeros_like(pad)

    mats, tams = (mat_a, mat_b, mat_c), (tam_a, tam_b, tam_c)
    offset = 0
    for kind, source in enumerate((mix_a, mix_b, mix_c)):
        width, rows_k, size = widths[kind], padded[kind], wide[kind]
        turned = pltpu.roll(pbias[...], pbias.shape[1] - offset, 1) if offset else pbias[...]
        offset += width
        row = lax.broadcasted_iota(jnp.int32, (size, size), 0)
        col = lax.broadcasted_iota(jnp.int32, (size, size), 1)
        for layer in range(LAYERS):
            pad[0:size, 0:size] = jnp.zeros((size, size), f32)
            pad[0:width, 0:width] = source[:, layer, :].astype(f32)
            biases = turned[layer : layer + 1, 0:size]
            column = jnp.sum(jnp.where(row == col, biases, 0.0), axis=1, keepdims=True)
            whole = jnp.where((col == width) & (row < width), column, pad[0:size, 0:size])
            mats[kind][layer] = whole[0:rows_k, 0:rows_k].astype(bf16)
            tams[kind][layer] = whole.T[0:rows_k, 0:rows_k].astype(bf16)

    def padded_image(value, kind):
        width, rows_k = widths[kind], padded[kind]
        edge = width // 8 * 8
        pad[edge:rows_k, :] = jnp.zeros((rows_k - edge, chans), f32)
        pad[0:width, :] = value
        return pad[0:rows_k, :]

    def live(kind, slot):
        return (slot < counts[section, kind]).astype(f32)

    for kind, slot, start in plan.segments:
        if slot == 0:
            fetches[kind].wait()
        xs[0, pl.ds(start, padded[kind]), :] = padded_image(raw_x[kind][:, slot, :].astype(f32), kind).astype(bf16)

    def blocks(kind):
        return [(low, min(BLOCK, padded[kind] - low)) for low in range(0, padded[kind], BLOCK)]

    def rows_from(low, shape):
        return lax.broadcasted_iota(jnp.int32, shape, 0) + low

    def mixer_input(kind, low, x, vec):
        z = vec[0:1] * x + vec[4:5]
        if low <= widths[kind] < low + x.shape[0]:
            z = jnp.where(rows_from(low, z.shape) == widths[kind], 1.0, z)
        return z.astype(bf16)

    def fold(value):
        return value.reshape(-1, 8, chans).sum(axis=0)

    def hidden(layer, chunk, begin, start, size):
        lanes = pl.ds(begin, CHUNK)
        bias = bias32[layer, :, lanes]
        product = nn(z2[pl.ds(start, size), :], w_in[layer, :, lanes])
        for low in range(0, size, BLOCK):
            high = min(low + BLOCK, size)
            a = product[low:high] + bias
            cdf = 0.5 + 0.5 * lax.erf(a * HALF_ROOT)
            slope = a * jnp.exp2(a * a * HALF_LOG2E) * PDF_SCALE
            part = pl.ds(start + low, high - low)
            hs[layer, chunk, part, :] = (a * cdf).astype(bf16)
            ds[layer, chunk, part, :] = (cdf + slope).astype(bf16)

    def forward(layer):
        vec = aff[layer]
        for kind, slot, start in plan.segments:
            span = pl.ds(start, padded[kind])
            for low, size in blocks(kind):
                part = pl.ds(start + low, size)
                z2[part, :] = mixer_input(kind, low, xs[layer, part, :].astype(f32), vec)
            product = nn(mats[kind][layer], z2[span, :])
            for low, size in blocks(kind):
                part = pl.ds(start + low, size)
                p = product[low : low + size]
                us[layer, part, :] = p.astype(bf16)
                x1 = (xs[layer, part, :].astype(f32) + vec[1:2] * p).astype(bf16)
                x1s[layer, part, :] = x1
                z2[part, :] = (vec[2:3] * x1.astype(f32) + vec[5:6]).astype(bf16)
                if layer < LAYERS - 1:
                    acc[part, :] = jnp.broadcast_to(vec[6:7], (size, chans))

        if layer == 0:
            fetches[6].wait()
            fetches[7].wait()

        if layer == LAYERS - 1:
            return
        for chunk in range(plan.chunks):
            second_weight = w_out[layer, pl.ds(chunk * CHUNK, CHUNK), :]
            for start, size in cuts(rows, 4):
                span = pl.ds(start, size)
                hidden(layer, chunk, chunk * CHUNK, start, size)
                acc[span, :] += nn(hs[layer, chunk, span, :], second_weight)

        for kind, slot, start in plan.segments:
            span = pl.ds(start, padded[kind])
            xs[layer + 1, span, :] = (x1s[layer, span, :].astype(f32) + vec[3:4] * acc[span, :]).astype(bf16)

    for layer in range(LAYERS):
        forward(layer)

    for kind, slot, start in plan.segments:
        if slot == 0:
            fetches[KINDS + kind].wait()
        cot = raw_c[kind][:, slot, :].astype(f32) * live(kind, slot)
        grad[pl.ds(start, padded[kind]), :] = padded_image(cot, kind).astype(bf16)

    pl.semaphore_wait(barrier, len(partners))

    base0 = core * plan.half
    base1 = base0 + first * plan.quarter
    base2 = base1 + second * plan.eighth
    base3 = base2 + deep * plan.last

    def at(ref, piece, start, size):
        return ref.at[piece, pl.ds(pl.multiple_of(start, ROWS), size)]

    def send(piece, hop, source, target, to):
        return pltpu.make_async_remote_copy(
            src_ref=source,
            dst_ref=target,
            send_sem=send_sem.at[hop],
            recv_sem=recv_sem.at[piece, hop],
            device_id=to,
            device_id_type=MESH,
        )

    def hop0(piece):
        return [send(piece, 0, at(own, piece, (1 - core) * plan.half, plan.half), land0.at[piece], core_to)]

    def hop1(piece):
        return [send(piece, 1, at(land0, piece, (1 - first) * plan.quarter, plan.quarter), land1.at[piece], first_to)]

    def hop2(piece):
        return [send(piece, 2, at(land1, piece, (1 - second) * plan.eighth, plan.eighth), land2.at[piece], second_to)]

    def hop3(piece):
        return [
            send(
                piece,
                3,
                at(land2, piece, lax.rem(deep + step, plan.depth) * plan.last, plan.last),
                land3.at[piece, step - 1],
                deep_to(step),
            )
            for step in range(1, plan.depth)
        ]

    def hop4(piece):
        spot = at(result, piece, base3, plan.last)
        return [send(piece, 4, spot, spot, deep_to(step)) for step in range(1, plan.depth)]

    def hop5(piece):
        spot = at(result, piece, base2, plan.eighth)
        return [send(piece, 5, spot, spot, second_to)]

    def hop6(piece):
        spot = at(result, piece, base1, plan.quarter)
        return [send(piece, 6, spot, spot, first_to)]

    def hop7(piece):
        spot = at(result, piece, base0, plan.half)
        return [send(piece, 7, spot, spot, core_to)]

    others = plan.last * (plan.depth - 1)

    def brought(piece, hop):
        whole = [
            land0.at[piece],
            land1.at[piece],
            land2.at[piece],
            land3.at[piece],
            at(result, piece, base2, others),
            at(result, piece, base2, plan.eighth),
            at(result, piece, base1, plan.quarter),
            at(result, piece, base0, plan.half),
        ][hop]
        return send(piece, hop, whole, whole, core_to)

    totals = [land0, land1, land2, land3, land3, land2, land1, land0]

    def start(copies):
        for copy in copies:
            copy.start()

    def get(ref, piece, start, size):
        return ref[piece, pl.ds(pl.multiple_of(start, ROWS), size), :].astype(f32)

    def add0(piece):
        land0[piece] = (land0[piece].astype(f32) + get(own, piece, base0, plan.half)).astype(bf16)

    def add1(piece):
        land1[piece] = (land1[piece].astype(f32) + get(land0, piece, first * plan.quarter, plan.quarter)).astype(bf16)

    def add2(piece):
        land2[piece] = (land2[piece].astype(f32) + get(land1, piece, second * plan.eighth, plan.eighth)).astype(bf16)

    def add3(piece):
        total = get(land2, piece, deep * plan.last, plan.last)
        for step in range(plan.depth - 1):
            total = total + land3[piece, step].astype(f32)
        result[piece, pl.ds(pl.multiple_of(base3, ROWS), plan.last), :] = total.astype(bf16)

    def nothing(piece):
        pass

    hops = [hop0, hop1, hop2, hop3, hop4, hop5, hop6, hop7]
    adds = [add0, add1, add2, add3, nothing, nothing, nothing, nothing]

    def tick(moment):
        for stage in range(len(hops) + 1):
            piece = moment - SLACK * stage

            @pl.when((piece >= 0) & (piece < plan.pieces))
            def _(stage=stage, piece=piece):
                if stage > 0:
                    brought(piece, stage - 1).wait_recv()
                    adds[stage - 1](piece)
                if stage < len(hops):
                    start(hops[stage](piece))

    def backward(turn):
        layer = LAYERS - 1 - turn
        vec = aff[layer]
        bias_sum = jnp.zeros((1, chans), f32)
        vecs[...] = jnp.zeros_like(vecs)
        for start in range(0, rows, LANES):
            span = pl.ds(start, min(LANES, rows - start))
            g = grad[span, :].astype(f32)
            dv = vec[3:4] * g
            bias_sum = bias_sum + col_sum(dv)
            low = dv.astype(bf16)
            dvr[span, :] = low
            dvt[:, span] = low.T
            z2t[:, span] = (vec[2:3] * x1s[layer, span, :].astype(f32) + vec[5:6]).astype(bf16).T
            acc[span, :] = jnp.zeros((span.size, chans), f32)

        def step(chunk, carry):
            lanes = pl.ds(pl.multiple_of(chunk * CHUNK, CHUNK), CHUNK)
            first_weight = w_in[layer, :, lanes]
            second_weight = w_out[layer, lanes, :]
            total = jnp.zeros((8, CHUNK), f32)
            for start, size in cuts(rows, 4):
                span = pl.ds(start, size)
                if layer == LAYERS - 1:
                    hidden(layer, chunk, pl.multiple_of(chunk * CHUNK, CHUNK), start, size)
                dh = nt(dvr[span, :], second_weight)
                for low in range(0, size, BLOCK):
                    high = min(low + BLOCK, size)
                    block_span = pl.ds(start + low, high - low)
                    dact = dh[low:high] * ds[layer, chunk, block_span, :].astype(f32)
                    total = total + dact.reshape(-1, 8, CHUNK).sum(axis=0)
                    da[block_span, :] = dact.astype(bf16)
                acc[span, :] += nt(da[span, :], first_weight)
            bgrad[:, lanes] = col_sum(total)
            piece = turn * plan.steps + chunk
            gin = nn(z2t[...], da[...]).astype(bf16)
            for part in range(CHUNK // LANES):
                own[piece, pl.ds(part * chans, chans), :] = gin[:, part * LANES : (part + 1) * LANES]
            gout = nn(dvt[...], hs[layer, chunk]).astype(bf16).T
            vecs[...] += (gout.astype(f32) * second_weight.astype(f32)).reshape(-1, 8, chans).sum(axis=0)
            for part in range(chans // LANES):
                own[piece, pl.ds(plan.half + part * CHUNK, CHUNK), :] = gout[:, part * LANES : (part + 1) * LANES]
            tick(piece)
            return carry

        lax.fori_loop(0, plan.chunks, step, 0)

        piece = turn * plan.steps + plan.chunks
        sums = [jnp.zeros((8, chans), f32) for _ in range(5)]
        for kind in range(KINDS):
            width, rows_k, size = widths[kind], padded[kind], wide[kind]
            mix_grad = jnp.zeros((rows_k, rows_k), f32)
            for seg_kind, slot, start in plan.segments:
                if seg_kind != kind:
                    continue
                span = pl.ds(start, rows_k)
                for low, count in blocks(kind):
                    part = pl.ds(start + low, count)
                    dz2 = acc[part, :]
                    sums[3] = sums[3] + fold(x1s[layer, part, :].astype(f32) * dz2)
                    sums[4] = sums[4] + fold(dz2)
                    low_g = (grad[part, :].astype(f32) + vec[2:3] * dz2).astype(bf16)
                    grad[part, :] = low_g
                    g1 = low_g.astype(f32)
                    sums[2] = sums[2] + fold(g1 * us[layer, part, :].astype(f32))
                    dvr[part, :] = (vec[1:2] * g1).astype(bf16)
                    z2[part, :] = mixer_input(kind, low, xs[layer, part, :].astype(f32), vec)
                mix_grad = mix_grad + nt(dvr[span, :], z2[span, :])
                product = nn(tams[kind][layer], dvr[span, :])
                for low, count in blocks(kind):
                    part = pl.ds(start + low, count)
                    dz = product[low : low + count]
                    if low + count > width:
                        dz = jnp.where(rows_from(low, dz.shape) < width, dz, 0.0)
                    sums[0] = sums[0] + fold(xs[layer, part, :].astype(f32) * dz)
                    sums[1] = sums[1] + fold(dz)
                    grad[part, :] = (grad[part, :].astype(f32) + vec[0:1] * dz).astype(bf16)
            pad[0:rows_k, 0:rows_k] = mix_grad
            if kind == KINDS - 1:
                for place in range(5):
                    pad[width + place : width + place + 1, :] = col_sum(sums[place])
                pad[width + 5 : width + 6, :] = (col_sum(vecs[...]) + vec[6:7] * bias_sum) / vec[3:4]
                pad[width + 6 : width + 7, :] = bias_sum
                for place in range(plan.hid // chans):
                    spot = width + 7 + place
                    pad[spot : spot + 1, :] = bgrad[:, place * chans : (place + 1) * chans]
            for part in range(size // LANES):
                place = plan.places[kind] + part * rows_k
                own[piece, pl.ds(place, rows_k), :] = pad[0:rows_k, part * LANES : (part + 1) * LANES].astype(bf16)
        tick(piece)

    for turn in range(LAYERS):
        backward(turn)

    def shown(buffer, kind, slot, start):
        return buffer[pl.ds(start, padded[kind]), :].astype(f32)[0 : widths[kind]]

    acc[...] = jnp.zeros_like(acc)

    def drain(moment, carry):
        tick(moment)

        @pl.when(moment == plan.pieces)
        def _():
            for kind, slot, begin in plan.segments:
                raw_c[kind][:, slot, :] = shown(grad, kind, slot, begin).astype(bf16)

        @pl.when(moment < plan.pieces + plan.chunks)
        def _():
            chunk = moment - plan.pieces
            lanes = pl.ds(pl.multiple_of(chunk * CHUNK, CHUNK), CHUNK)
            acc[...] += nn(hs[LAYERS - 1, chunk], w_out[LAYERS - 1, lanes, :])

        @pl.when(moment == plan.pieces + plan.chunks)
        def _():
            vec = aff[LAYERS - 1]
            for kind, slot, begin in plan.segments:
                span = pl.ds(begin, padded[kind])
                y = (x1s[LAYERS - 1, span, :].astype(f32) + vec[3:4] * (acc[span, :] + vec[6:7])).astype(bf16)
                raw_x[kind][:, slot, :] = (y.astype(f32) * live(kind, slot)).astype(bf16)[0 : widths[kind]]

        return carry

    lax.fori_loop(plan.pieces, plan.pieces + SLACK * len(hops), drain, 0)

    for hop, total in enumerate(totals):
        pltpu.make_async_remote_copy(
            src_ref=total,
            dst_ref=total,
            send_sem=send_sem.at[hop],
            recv_sem=recv_sem.at[0, hop],
            device_id=core_to,
            device_id_type=MESH,
        ).wait_send()


def body(plan, *args):
    slots, chans, hid, rows = plan.slots, plan.chans, plan.hid, plan.rows
    images = [(width, slots, chans) for width in plan.widths]
    anywhere = pl.BlockSpec(memory_space=pl.ANY)
    vmem = pl.BlockSpec(memory_space=pltpu.VMEM)
    in_specs = [anywhere] * 6 + [pl.BlockSpec(memory_space=pltpu.SMEM)] + [vmem] * 7 + [anywhere] * 2
    (
        *pictures,
        live_counts,
        scales,
        shifts,
        mix_a,
        mix_b,
        mix_c,
        patch_bias,
        weight_in,
        bias_in,
        weight_out,
    ) = args
    scratch = [
        pltpu.VMEM((LAYERS, chans, hid), bf16),
        pltpu.VMEM((LAYERS, hid, chans), bf16),
        pltpu.VMEM((max(plan.wide), chans), f32),
        pltpu.VMEM((8, up(patch_bias.shape[1], LANES)), f32),
        pltpu.VMEM((LAYERS, 8, chans), f32),
        pltpu.VMEM((LAYERS, 1, hid), f32),
    ]
    scratch += [pltpu.VMEM((LAYERS, size, size), bf16) for size in plan.padded * 2]
    scratch += [
        pltpu.VMEM((LAYERS, rows, chans), bf16),
        pltpu.VMEM((LAYERS, rows, chans), bf16),
        pltpu.VMEM((LAYERS, rows, chans), bf16),
        pltpu.VMEM((LAYERS, plan.chunks, rows, CHUNK), bf16),
        pltpu.VMEM((LAYERS, plan.chunks, rows, CHUNK), bf16),
        pltpu.VMEM((rows, chans), bf16),
        pltpu.VMEM((rows, chans), f32),
        pltpu.VMEM((rows, chans), bf16),
        pltpu.VMEM((rows, chans), bf16),
        pltpu.VMEM((chans, rows), bf16),
        pltpu.VMEM((chans, rows), bf16),
        pltpu.VMEM((rows, CHUNK), bf16),
        pltpu.VMEM((8, chans), f32),
        pltpu.VMEM((1, hid), f32),
        pltpu.VMEM((plan.pieces, plan.size, LANES), bf16),
        pltpu.VMEM((plan.pieces, plan.half, LANES), bf16),
        pltpu.VMEM((plan.pieces, plan.quarter, LANES), bf16),
        pltpu.VMEM((plan.pieces, plan.eighth, LANES), bf16),
        pltpu.VMEM((plan.pieces, plan.depth - 1, plan.last, LANES), bf16),
        pltpu.SemaphoreType.DMA((8,)),
        pltpu.SemaphoreType.DMA((8,)),
        pltpu.SemaphoreType.DMA((plan.pieces, 8)),
    ]
    out_shape = [pltpu.VMEM(shape, bf16) for shape in images * 2]
    stays = pltpu.VMEM if plan.outer == 1 else jax.ShapeDtypeStruct
    out_shape.append(stays((plan.pieces, plan.size, LANES), bf16))
    views = [picture.transpose(1, 0, 2) for picture in pictures]
    mixes = [mix.transpose(1, 0, 2) for mix in (mix_a, mix_b, mix_c)]
    *shown, sums = pl.pallas_call(
        functools.partial(kernel, plan),
        out_shape=out_shape,
        in_specs=in_specs,
        out_specs=[vmem] * 7,
        scratch_shapes=scratch,
        compiler_params=pltpu.CompilerParams(
            collective_id=0, has_side_effects=True, vmem_limit_bytes=(55 if plan.outer == 1 else 60) * 1024 * 1024
        ),
    )(*views, live_counts, scales, shifts.transpose(1, 0, 2), *mixes, patch_bias, bias_in, weight_in, weight_out)
    if plan.outer > 1:
        ring = 2 * plan.depth
        groups = [[low + ring * high for high in range(plan.outer)] for low in range(ring)]
        sums = lax.psum(sums, "dp", axis_index_groups=groups)
    finals = [jax.ShapeDtypeStruct(shape, bf16) for shape in images * 2]
    finals += [
        jax.ShapeDtypeStruct(shape, f32)
        for shape in [(LAYERS, 4, chans), (3, LAYERS, chans)]
        + [(width, LAYERS, width) for width in plan.widths]
        + [(LAYERS, sum(plan.widths)), (LAYERS, chans, hid), (LAYERS, hid), (LAYERS, hid, chans)]
    ]
    out = pl.pallas_call(
        functools.partial(unpack, plan),
        out_shape=finals,
        in_specs=[vmem] * 7,
        out_specs=[anywhere] * 6 + [vmem] * 2 + [anywhere] * 3 + [vmem, anywhere, vmem, anywhere],
        scratch_shapes=[
            pltpu.VMEM((LAYERS, chans, hid), f32),
            pltpu.VMEM((LAYERS, hid, chans), f32),
            pltpu.VMEM((LAYERS, max(plan.wide), chans), f32),
            *(pltpu.VMEM((width, LAYERS, width), f32) for width in plan.widths),
            pltpu.SemaphoreType.DMA((6,)),
            pltpu.SemaphoreType.DMA((KINDS,)),
            pltpu.SemaphoreType.DMA((LAYERS, plan.chunks, 2)),
        ],
        compiler_params=pltpu.CompilerParams(vmem_limit_bytes=24 * 1024 * 1024),
    )(*shown, sums)
    order = [value.transpose(1, 0, 2) for value in out[:6]]
    return (*order, out[6], out[7].transpose(1, 0, 2), *(mix.transpose(1, 0, 2) for mix in out[8:11]), *out[11:])


def unpack(
    plan, ia, ib, ic, ja, jb, jc, held,
    oa, ob, oc, ga, gb, gc, g_scales, g_shifts, g_mix_a, g_mix_b, g_mix_c, g_patch, g_in, g_bias, g_out,
    wide_in, wide_out, square, mix_a, mix_b, mix_c, copy_sem, mix_sem, out_sem,
):
    chans, chunks = plan.chans, plan.chunks
    moves = []
    for place, (source, target) in enumerate(zip((ia, ib, ic, ja, jb, jc), (oa, ob, oc, ga, gb, gc))):
        moves.append(pltpu.make_async_copy(source, target, copy_sem.at[place]))
    for move in moves:
        move.start()
    g_patch[...] = jnp.zeros_like(g_patch)
    firsts = [(LAYERS - 1 - layer) * plan.steps for layer in range(LAYERS)]
    offset = 0
    for kind, (stage, target) in enumerate(zip((mix_a, mix_b, mix_c), (g_mix_a, g_mix_b, g_mix_c))):
        width, rows_k, size = plan.widths[kind], plan.padded[kind], plan.wide[kind]
        for layer in range(LAYERS):
            for part in range(size // LANES):
                spot = pl.ds(plan.places[kind] + part * rows_k, rows_k)
                value = held[firsts[layer] + chunks, spot, :].astype(f32)
                square[layer, 0:rows_k, part * LANES : (part + 1) * LANES] = value
            whole = square[layer, 0:rows_k, 0:size]
            stage[:, layer, :] = whole[0:width, 0:width]
            row = lax.broadcasted_iota(jnp.int32, (rows_k, size), 0)
            col = lax.broadcasted_iota(jnp.int32, (rows_k, size), 1)
            column = jnp.sum(jnp.where(col == width, whole, 0.0), axis=1, keepdims=True)
            turned = jnp.sum(jnp.where((row == col) & (row < width), column, 0.0), axis=0, keepdims=True)
            g_patch[layer : layer + 1, offset : offset + width] = turned[:, 0:width]
        moves.append(pltpu.make_async_copy(stage, target, mix_sem.at[kind]))
        moves[-1].start()
        offset += width
    for layer in reversed(range(LAYERS)):
        for step in range(chunks):
            lanes = pl.ds(step * CHUNK, CHUNK)
            piece = firsts[layer] + step
            for part in range(CHUNK // LANES):
                spot = pl.ds(step * CHUNK + part * LANES, LANES)
                wide_in[layer, :, spot] = held[piece, pl.ds(part * chans, chans), :].astype(f32)
            for part in range(chans // LANES):
                spot = pl.ds(part * LANES, LANES)
                wide_out[layer, lanes, spot] = held[piece, pl.ds(plan.half + part * CHUNK, CHUNK), :].astype(f32)
            for place, (source, target) in enumerate(
                ((wide_in.at[layer, :, lanes], g_in.at[layer, :, lanes]), (wide_out.at[layer, lanes], g_out.at[layer, lanes]))
            ):
                moves.append(pltpu.make_async_copy(source, target, out_sem.at[layer, step, place]))
                moves[-1].start()
        width = plan.widths[KINDS - 1]
        small = square[layer, width : width + 7 + plan.hid // chans, :]
        for place, row in enumerate((0, 2, 3, 5)):
            g_scales[layer, place : place + 1, :] = small[row : row + 1]
        for place, row in enumerate((1, 4, 6)):
            g_shifts[place, layer : layer + 1, :] = small[row : row + 1]
        for place in range(plan.hid // chans):
            g_bias[layer : layer + 1, place * chans : (place + 1) * chans] = small[7 + place : 8 + place]
    for move in moves:
        move.wait()


def solution(mesh):
    sections, dp = mesh.shape["section"], mesh.shape["dp"]

    def run(*args):
        images, weight_in = args[:3], args[13]
        slots = images[0].shape[0] // (sections * dp)
        widths = tuple(image.shape[1] for image in images)
        plan = Plan(sections, dp, slots, widths, weight_in.shape[1], weight_in.shape[2])
        split_in = P("dp", None, None)
        split_out = P(("dp", "section"), None, None)
        in_specs = (split_in,) * 6 + (P("dp", None),) + (P(),) * 9
        out_specs = (split_out,) * 6 + (P(),) * 9
        whole = jax.shard_map(
            functools.partial(body, plan), mesh=mesh, in_specs=in_specs, out_specs=out_specs, check_vma=False
        )
        return whole(*args)

    return run
```

```python
import functools

import jax
import jax.numpy as jnp
from jax import lax
from jax.experimental import pallas as pl
from jax.experimental.pallas import tpu as pltpu
from jax.sharding import PartitionSpec as P

MESH = pl.DeviceIdType.MESH
f32 = jnp.float32
bf16 = jnp.bfloat16
LAYERS = 2
KINDS = 3
LANES = 128
ROWS = 16
CHUNK = 256
DELAYS = (0, 1, 3, 5, 7, 9, 11, 13, 14)
BLOCK = 32
HALF_LOG2E = -0.7213475204444817
HALF_ROOT = 0.7071067811865476
PDF_SCALE = 0.3989422804014327


def up(value, unit):
    return -(-value // unit) * unit


def nt(left, right):
    return lax.dot_general(left, right, (((1,), (1,)), ((), ())), preferred_element_type=f32)


def nn(left, right):
    return jnp.dot(left, right, preferred_element_type=f32)


def col_sum(value):
    return jnp.sum(value, axis=0, keepdims=True)


def cuts(total, pieces):
    tiles = total // ROWS
    marks = [tiles * k // pieces * ROWS for k in range(pieces + 1)]
    return [(marks[k], marks[k + 1] - marks[k]) for k in range(pieces)]


class Plan:
    def __init__(self, sections, dp, slots, widths, chans, hid):
        self.sections, self.dp, self.slots, self.widths, self.chans, self.hid = sections, dp, slots, widths, chans, hid
        self.padded = tuple(up(width + 1, ROWS) for width in widths)
        self.wide = tuple(up(rows, LANES) for rows in self.padded)
        self.segments = []
        start = 0
        for kind in range(KINDS):
            for slot in range(slots):
                self.segments.append((kind, slot, start))
                start += self.padded[kind]
        self.rows = start
        self.chunks = hid // CHUNK
        self.steps = self.chunks + 1
        self.pieces = LAYERS * self.steps
        self.depth = min(4, dp // 2)
        self.outer = dp // (2 * self.depth)
        self.size = 2 * chans * CHUNK // LANES
        self.half, self.quarter, self.eighth = self.size // 2, self.size // 4, self.size // 8
        self.last = self.eighth // self.depth
        self.places, place = {}, 0
        for kind in reversed(range(KINDS)):
            self.places[kind] = place
            place += self.padded[kind] * (self.wide[kind] // LANES)
        assert place <= self.size and self.last % ROWS == 0 and sections == 4 and self.depth > 1


def kernel(
    plan,
    xa, xb, xc, ca, cb, cc, counts, scales, shifts, mix_a, mix_b, mix_c, patch_bias, bias_in, w_in_hbm, w_out_hbm,
    oa, ob, oc, ga, gb, gc, result,
    w_in, w_out, pad, pbias, aff, bias32, mat_a, mat_b, mat_c, tam_a, tam_b, tam_c,
    xs, x1s, us, hs, ds, z2, acc, grad, dvr, dvt, z2t, da, vecs, bgrad,
    own, land0, land1, land2, land3,
    io_sem, send_sem, recv_sem,
):
    widths, padded, wide = plan.widths, plan.padded, plan.wide
    slots, chans, rows = plan.slots, plan.chans, plan.rows
    section = lax.axis_index("section")
    dp = lax.axis_index("dp")
    core = lax.rem(dp, 2)
    deep = lax.rem(lax.div(dp, 2), plan.depth)
    block = dp - lax.rem(dp, 2 * plan.depth)
    bit0, bit1 = lax.rem(section, 2), lax.div(section, 2)
    first = jnp.where(core == 0, bit0, bit1)
    second = jnp.where(core == 0, bit1, bit0)
    flip0 = section + 1 - 2 * bit0
    flip1 = section + 2 - 4 * bit1
    first_to = (jnp.where(core == 0, flip0, flip1), dp)
    second_to = (jnp.where(core == 0, flip1, flip0), dp)
    core_to = (section, dp + 1 - 2 * core)

    def deep_to(step):
        return (section, block + lax.rem(deep + step, plan.depth) * 2 + core)

    partners = [core_to, first_to, second_to] + [deep_to(step) for step in range(1, plan.depth)]
    barrier = pltpu.get_barrier_semaphore()
    for partner in partners:
        pl.semaphore_signal(barrier, inc=1, device_id=partner, device_id_type=MESH)

    raw_x, raw_c = (oa, ob, oc), (ga, gb, gc)
    fetches = []
    mine = pl.ds(pl.multiple_of(section * slots, slots), slots)
    pairs = list(zip((xa, xb, xc), raw_x)) + list(zip((ca, cb, cc), raw_c))
    for place, (source, target) in enumerate(pairs):
        fetches.append(pltpu.make_async_copy(source.at[:, mine, :], target, io_sem.at[place]))
    fetches.append(pltpu.make_async_copy(w_in_hbm, w_in, io_sem.at[6]))
    fetches.append(pltpu.make_async_copy(w_out_hbm, w_out, io_sem.at[7]))
    for fetch in fetches[:3] + fetches[6:] + fetches[3:6]:
        fetch.start()

    for layer in range(LAYERS):
        aff[layer, 0:4, :] = scales[layer].astype(f32)
        aff[layer, 4:7, :] = shifts[:, layer, :].astype(f32)
        bias32[layer, :, :] = bias_in[...].astype(f32)[layer : layer + 1]
    pbias[...] = jnp.zeros_like(pbias)
    pbias[0:LAYERS, 0 : patch_bias.shape[1]] = patch_bias[...].astype(f32)
    pad[...] = jnp.zeros_like(pad)

    mats, tams = (mat_a, mat_b, mat_c), (tam_a, tam_b, tam_c)
    offset = 0
    for kind, source in enumerate((mix_a, mix_b, mix_c)):
        width, rows_k, size = widths[kind], padded[kind], wide[kind]
        turned = pltpu.roll(pbias[...], pbias.shape[1] - offset, 1) if offset else pbias[...]
        offset += width
        row = lax.broadcasted_iota(jnp.int32, (size, size), 0)
        col = lax.broadcasted_iota(jnp.int32, (size, size), 1)
        for layer in range(LAYERS):
            pad[0:size, 0:size] = jnp.zeros((size, size), f32)
            pad[0:width, 0:width] = source[:, layer, :].astype(f32)
            biases = turned[layer : layer + 1, 0:size]
            column = jnp.sum(jnp.where(row == col, biases, 0.0), axis=1, keepdims=True)
            whole = jnp.where((col == width) & (row < width), column, pad[0:size, 0:size])
            mats[kind][layer] = whole[0:rows_k, 0:rows_k].astype(bf16)
            tams[kind][layer] = whole.T[0:rows_k, 0:rows_k].astype(bf16)

    def padded_image(value, kind):
        width, rows_k = widths[kind], padded[kind]
        edge = width // 8 * 8
        pad[edge:rows_k, :] = jnp.zeros((rows_k - edge, chans), f32)
        pad[0:width, :] = value
        return pad[0:rows_k, :]

    def live(kind, slot):
        return (slot < counts[section, kind]).astype(f32)

    for kind, slot, start in plan.segments:
        if slot == 0:
            fetches[kind].wait()
        xs[0, pl.ds(start, padded[kind]), :] = padded_image(raw_x[kind][:, slot, :].astype(f32), kind).astype(bf16)

    def ones_row(kind, value):
        row = lax.broadcasted_iota(jnp.int32, value.shape, 0)
        return jnp.where(row == widths[kind], 1.0, value).astype(bf16)

    def forward(layer):
        vec = aff[layer]
        for kind, slot, start in plan.segments:
            span = pl.ds(start, padded[kind])
            x = xs[layer, span, :].astype(f32)
            z = ones_row(kind, vec[0:1] * x + vec[4:5])
            p = nn(mats[kind][layer], z)
            us[layer, span, :] = p.astype(bf16)
            x1 = (x + vec[1:2] * p).astype(bf16)
            x1s[layer, span, :] = x1
            z2[span, :] = (vec[2:3] * x1.astype(f32) + vec[5:6]).astype(bf16)
            if layer < LAYERS - 1:
                acc[span, :] = jnp.broadcast_to(vec[6:7], (padded[kind], chans))

        if layer == 0:
            fetches[6].wait()
            fetches[7].wait()

        for chunk in range(plan.chunks):
            lanes = pl.ds(chunk * CHUNK, CHUNK)
            bias = bias32[layer, :, lanes]
            first_weight = w_in[layer, :, lanes]
            second_weight = w_out[layer, lanes, :]
            for start, size in cuts(rows, 4):
                span = pl.ds(start, size)
                product = nn(z2[span, :], first_weight)
                for low in range(0, size, BLOCK):
                    high = min(low + BLOCK, size)
                    a = product[low:high] + bias
                    cdf = 0.5 + 0.5 * lax.erf(a * HALF_ROOT)
                    slope = a * jnp.exp2(a * a * HALF_LOG2E) * PDF_SCALE
                    block_span = pl.ds(start + low, high - low)
                    hs[layer, chunk, block_span, :] = (a * cdf).astype(bf16)
                    ds[layer, chunk, block_span, :] = (cdf + slope).astype(bf16)
                if layer < LAYERS - 1:
                    acc[span, :] += nn(hs[layer, chunk, span, :], second_weight)

        if layer < LAYERS - 1:
            for kind, slot, start in plan.segments:
                span = pl.ds(start, padded[kind])
                xs[layer + 1, span, :] = (x1s[layer, span, :].astype(f32) + vec[3:4] * acc[span, :]).astype(bf16)

    for layer in range(LAYERS):
        forward(layer)

    for kind, slot, start in plan.segments:
        if slot == 0:
            fetches[KINDS + kind].wait()
        cot = raw_c[kind][:, slot, :].astype(f32) * live(kind, slot)
        grad[pl.ds(start, padded[kind]), :] = padded_image(cot, kind).astype(bf16)

    pl.semaphore_wait(barrier, len(partners))

    base0 = core * plan.half
    base1 = base0 + first * plan.quarter
    base2 = base1 + second * plan.eighth
    base3 = base2 + deep * plan.last

    def at(ref, piece, start, size):
        return ref.at[piece, pl.ds(pl.multiple_of(start, ROWS), size)]

    def send(piece, hop, source, target, to):
        return pltpu.make_async_remote_copy(
            src_ref=source,
            dst_ref=target,
            send_sem=send_sem.at[hop],
            recv_sem=recv_sem.at[piece, hop],
            device_id=to,
            device_id_type=MESH,
        )

    def hop0(piece):
        return [send(piece, 0, at(own, piece, (1 - core) * plan.half, plan.half), land0.at[piece], core_to)]

    def hop1(piece):
        return [send(piece, 1, at(land0, piece, (1 - first) * plan.quarter, plan.quarter), land1.at[piece], first_to)]

    def hop2(piece):
        return [send(piece, 2, at(land1, piece, (1 - second) * plan.eighth, plan.eighth), land2.at[piece], second_to)]

    def hop3(piece):
        return [
            send(
                piece,
                3,
                at(land2, piece, lax.rem(deep + step, plan.depth) * plan.last, plan.last),
                land3.at[piece, step - 1],
                deep_to(step),
            )
            for step in range(1, plan.depth)
        ]

    def hop4(piece):
        spot = at(result, piece, base3, plan.last)
        return [send(piece, 4, spot, spot, deep_to(step)) for step in range(1, plan.depth)]

    def hop5(piece):
        spot = at(result, piece, base2, plan.eighth)
        return [send(piece, 5, spot, spot, second_to)]

    def hop6(piece):
        spot = at(result, piece, base1, plan.quarter)
        return [send(piece, 6, spot, spot, first_to)]

    def hop7(piece):
        spot = at(result, piece, base0, plan.half)
        return [send(piece, 7, spot, spot, core_to)]

    others = plan.last * (plan.depth - 1)

    def brought(piece, hop):
        whole = [
            land0.at[piece],
            land1.at[piece],
            land2.at[piece],
            land3.at[piece],
            at(result, piece, base2, others),
            at(result, piece, base2, plan.eighth),
            at(result, piece, base1, plan.quarter),
            at(result, piece, base0, plan.half),
        ][hop]
        return send(piece, hop, whole, whole, core_to)

    totals = [land0, land1, land2, land3, land3, land2, land1, land0]

    def start(copies):
        for copy in copies:
            copy.start()

    def get(ref, piece, start, size):
        return ref[piece, pl.ds(pl.multiple_of(start, ROWS), size), :].astype(f32)

    def add0(piece):
        land0[piece] = (land0[piece].astype(f32) + get(own, piece, base0, plan.half)).astype(bf16)

    def add1(piece):
        land1[piece] = (land1[piece].astype(f32) + get(land0, piece, first * plan.quarter, plan.quarter)).astype(bf16)

    def add2(piece):
        land2[piece] = (land2[piece].astype(f32) + get(land1, piece, second * plan.eighth, plan.eighth)).astype(bf16)

    def add3(piece):
        total = get(land2, piece, deep * plan.last, plan.last)
        for step in range(plan.depth - 1):
            total = total + land3[piece, step].astype(f32)
        result[piece, pl.ds(pl.multiple_of(base3, ROWS), plan.last), :] = total.astype(bf16)

    def nothing(piece):
        pass

    hops = [hop0, hop1, hop2, hop3, hop4, hop5, hop6, hop7]
    adds = [add0, add1, add2, add3, nothing, nothing, nothing, nothing]

    def tick(moment):
        for stage in range(len(hops) + 1):
            piece = moment - DELAYS[stage]

            @pl.when((piece >= 0) & (piece < plan.pieces))
            def _(stage=stage, piece=piece):
                if stage > 0:
                    brought(piece, stage - 1).wait_recv()
                    adds[stage - 1](piece)
                if stage < len(hops):
                    start(hops[stage](piece))

    def backward(turn):
        layer = LAYERS - 1 - turn
        vec = aff[layer]
        bias_sum = jnp.zeros((1, chans), f32)
        vecs[...] = jnp.zeros_like(vecs)
        for start in range(0, rows, LANES):
            span = pl.ds(start, min(LANES, rows - start))
            g = grad[span, :].astype(f32)
            dv = vec[3:4] * g
            bias_sum = bias_sum + col_sum(dv)
            low = dv.astype(bf16)
            dvr[span, :] = low
            dvt[:, span] = low.T
            z2t[:, span] = (vec[2:3] * x1s[layer, span, :].astype(f32) + vec[5:6]).astype(bf16).T
            acc[span, :] = jnp.zeros((span.size, chans), f32)

        def step(chunk, carry):
            lanes = pl.ds(pl.multiple_of(chunk * CHUNK, CHUNK), CHUNK)
            first_weight = w_in[layer, :, lanes]
            second_weight = w_out[layer, lanes, :]
            total = jnp.zeros((8, CHUNK), f32)
            for start, size in cuts(rows, 4):
                span = pl.ds(start, size)
                dh = nt(dvr[span, :], second_weight)
                for low in range(0, size, BLOCK):
                    high = min(low + BLOCK, size)
                    block_span = pl.ds(start + low, high - low)
                    dact = dh[low:high] * ds[layer, chunk, block_span, :].astype(f32)
                    total = total + dact.reshape(-1, 8, CHUNK).sum(axis=0)
                    da[block_span, :] = dact.astype(bf16)
                acc[span, :] += nt(da[span, :], first_weight)
            bgrad[:, lanes] = col_sum(total)
            piece = turn * plan.steps + chunk
            gin = nn(z2t[...], da[...]).astype(bf16)
            for part in range(CHUNK // LANES):
                own[piece, pl.ds(part * chans, chans), :] = gin[:, part * LANES : (part + 1) * LANES]
            gout = nn(dvt[...], hs[layer, chunk]).astype(bf16).T
            vecs[...] += (gout.astype(f32) * second_weight.astype(f32)).reshape(-1, 8, chans).sum(axis=0)
            for part in range(chans // LANES):
                own[piece, pl.ds(plan.half + part * CHUNK, CHUNK), :] = gout[:, part * LANES : (part + 1) * LANES]
            tick(piece)
            return carry

        lax.fori_loop(0, plan.chunks, step, 0)

        piece = turn * plan.steps + plan.chunks
        sums = [jnp.zeros((1, chans), f32) for _ in range(5)]
        for kind in range(KINDS):
            width, rows_k, size = widths[kind], padded[kind], wide[kind]
            mix_grad = jnp.zeros((rows_k, rows_k), f32)
            for seg_kind, slot, start in plan.segments:
                if seg_kind != kind:
                    continue
                span = pl.ds(start, rows_k)
                dz2 = acc[span, :]
                sums[3] = sums[3] + col_sum(x1s[layer, span, :].astype(f32) * dz2)
                sums[4] = sums[4] + col_sum(dz2)
                g1 = (grad[span, :].astype(f32) + vec[2:3] * dz2).astype(bf16).astype(f32)
                sums[2] = sums[2] + col_sum(g1 * us[layer, span, :].astype(f32))
                dp = (vec[1:2] * g1).astype(bf16)
                x = xs[layer, span, :].astype(f32)
                z = ones_row(kind, vec[0:1] * x + vec[4:5])
                mix_grad = mix_grad + nt(dp, z)
                dz = nn(tams[kind][layer], dp)
                row = lax.broadcasted_iota(jnp.int32, dz.shape, 0)
                dz = jnp.where(row < width, dz, 0.0)
                sums[0] = sums[0] + col_sum(x * dz)
                sums[1] = sums[1] + col_sum(dz)
                grad[span, :] = (g1 + vec[0:1] * dz).astype(bf16)
            pad[0:rows_k, 0:rows_k] = mix_grad
            if kind == KINDS - 1:
                for place in range(5):
                    pad[width + place : width + place + 1, :] = sums[place]
                pad[width + 5 : width + 6, :] = (col_sum(vecs[...]) + vec[6:7] * bias_sum) / vec[3:4]
                pad[width + 6 : width + 7, :] = bias_sum
                for place in range(plan.hid // chans):
                    spot = width + 7 + place
                    pad[spot : spot + 1, :] = bgrad[:, place * chans : (place + 1) * chans]
            for part in range(size // LANES):
                place = plan.places[kind] + part * rows_k
                own[piece, pl.ds(place, rows_k), :] = pad[0:rows_k, part * LANES : (part + 1) * LANES].astype(bf16)
        tick(piece)

    for turn in range(LAYERS):
        backward(turn)

    def shown(buffer, kind, slot, start):
        return buffer[pl.ds(start, padded[kind]), :].astype(f32)[0 : widths[kind]]

    acc[...] = jnp.zeros_like(acc)

    def drain(moment, carry):
        tick(moment)

        @pl.when(moment == plan.pieces)
        def _():
            for kind, slot, begin in plan.segments:
                raw_c[kind][:, slot, :] = shown(grad, kind, slot, begin).astype(bf16)

        @pl.when(moment < plan.pieces + plan.chunks)
        def _():
            chunk = moment - plan.pieces
            lanes = pl.ds(pl.multiple_of(chunk * CHUNK, CHUNK), CHUNK)
            acc[...] += nn(hs[LAYERS - 1, chunk], w_out[LAYERS - 1, lanes, :])

        @pl.when(moment == plan.pieces + plan.chunks)
        def _():
            vec = aff[LAYERS - 1]
            for kind, slot, begin in plan.segments:
                span = pl.ds(begin, padded[kind])
                y = (x1s[LAYERS - 1, span, :].astype(f32) + vec[3:4] * (acc[span, :] + vec[6:7])).astype(bf16)
                raw_x[kind][:, slot, :] = (y.astype(f32) * live(kind, slot)).astype(bf16)[0 : widths[kind]]

        return carry

    lax.fori_loop(plan.pieces, plan.pieces + DELAYS[-1], drain, 0)

    for hop, total in enumerate(totals):
        pltpu.make_async_remote_copy(
            src_ref=total,
            dst_ref=total,
            send_sem=send_sem.at[hop],
            recv_sem=recv_sem.at[0, hop],
            device_id=core_to,
            device_id_type=MESH,
        ).wait_send()


def body(plan, *args):
    slots, chans, hid, rows = plan.slots, plan.chans, plan.hid, plan.rows
    images = [(width, slots, chans) for width in plan.widths]
    anywhere = pl.BlockSpec(memory_space=pl.ANY)
    vmem = pl.BlockSpec(memory_space=pltpu.VMEM)
    in_specs = [anywhere] * 6 + [pl.BlockSpec(memory_space=pltpu.SMEM)] + [vmem] * 7 + [anywhere] * 2
    (
        *pictures,
        live_counts,
        scales,
        shifts,
        mix_a,
        mix_b,
        mix_c,
        patch_bias,
        weight_in,
        bias_in,
        weight_out,
    ) = args
    scratch = [
        pltpu.VMEM((LAYERS, chans, hid), bf16),
        pltpu.VMEM((LAYERS, hid, chans), bf16),
        pltpu.VMEM((max(plan.wide), chans), f32),
        pltpu.VMEM((8, up(patch_bias.shape[1], LANES)), f32),
        pltpu.VMEM((LAYERS, 8, chans), f32),
        pltpu.VMEM((LAYERS, 1, hid), f32),
    ]
    scratch += [pltpu.VMEM((LAYERS, size, size), bf16) for size in plan.padded * 2]
    scratch += [
        pltpu.VMEM((LAYERS, rows, chans), bf16),
        pltpu.VMEM((LAYERS, rows, chans), bf16),
        pltpu.VMEM((LAYERS, rows, chans), bf16),
        pltpu.VMEM((LAYERS, plan.chunks, rows, CHUNK), bf16),
        pltpu.VMEM((LAYERS, plan.chunks, rows, CHUNK), bf16),
        pltpu.VMEM((rows, chans), bf16),
        pltpu.VMEM((rows, chans), f32),
        pltpu.VMEM((rows, chans), bf16),
        pltpu.VMEM((rows, chans), bf16),
        pltpu.VMEM((chans, rows), bf16),
        pltpu.VMEM((chans, rows), bf16),
        pltpu.VMEM((rows, CHUNK), bf16),
        pltpu.VMEM((8, chans), f32),
        pltpu.VMEM((1, hid), f32),
        pltpu.VMEM((plan.pieces, plan.size, LANES), bf16),
        pltpu.VMEM((plan.pieces, plan.half, LANES), bf16),
        pltpu.VMEM((plan.pieces, plan.quarter, LANES), bf16),
        pltpu.VMEM((plan.pieces, plan.eighth, LANES), bf16),
        pltpu.VMEM((plan.pieces, plan.depth - 1, plan.last, LANES), bf16),
        pltpu.SemaphoreType.DMA((8,)),
        pltpu.SemaphoreType.DMA((8,)),
        pltpu.SemaphoreType.DMA((plan.pieces, 8)),
    ]
    out_shape = [pltpu.VMEM(shape, bf16) for shape in images * 2]
    stays = pltpu.VMEM if plan.outer == 1 else jax.ShapeDtypeStruct
    out_shape.append(stays((plan.pieces, plan.size, LANES), bf16))
    views = [picture.transpose(1, 0, 2) for picture in pictures]
    mixes = [mix.transpose(1, 0, 2) for mix in (mix_a, mix_b, mix_c)]
    *shown, sums = pl.pallas_call(
        functools.partial(kernel, plan),
        out_shape=out_shape,
        in_specs=in_specs,
        out_specs=[vmem] * 7,
        scratch_shapes=scratch,
        compiler_params=pltpu.CompilerParams(
            collective_id=0, has_side_effects=True, vmem_limit_bytes=(55 if plan.outer == 1 else 60) * 1024 * 1024
        ),
    )(*views, live_counts, scales, shifts.transpose(1, 0, 2), *mixes, patch_bias, bias_in, weight_in, weight_out)
    if plan.outer > 1:
        ring = 2 * plan.depth
        groups = [[low + ring * high for high in range(plan.outer)] for low in range(ring)]
        sums = lax.psum(sums, "dp", axis_index_groups=groups)
    finals = [jax.ShapeDtypeStruct(shape, bf16) for shape in images * 2]
    finals += [
        jax.ShapeDtypeStruct(shape, f32)
        for shape in [(LAYERS, 4, chans), (3, LAYERS, chans)]
        + [(width, LAYERS, width) for width in plan.widths]
        + [(LAYERS, sum(plan.widths)), (LAYERS, chans, hid), (LAYERS, hid), (LAYERS, hid, chans)]
    ]
    out = pl.pallas_call(
        functools.partial(unpack, plan),
        out_shape=finals,
        in_specs=[vmem] * 7,
        out_specs=[anywhere] * 6 + [vmem] * 6 + [anywhere, vmem, anywhere],
        scratch_shapes=[
            pltpu.VMEM((LAYERS, chans, hid), f32),
            pltpu.VMEM((LAYERS, hid, chans), f32),
            pltpu.VMEM((max(plan.wide), chans), f32),
            pltpu.SemaphoreType.DMA((6,)),
            pltpu.SemaphoreType.DMA((LAYERS, plan.chunks, 2)),
        ],
        compiler_params=pltpu.CompilerParams(vmem_limit_bytes=24 * 1024 * 1024),
    )(*shown, sums)
    order = [value.transpose(1, 0, 2) for value in out[:6]]
    return (*order, out[6], out[7].transpose(1, 0, 2), *(mix.transpose(1, 0, 2) for mix in out[8:11]), *out[11:])


def unpack(
    plan, ia, ib, ic, ja, jb, jc, held,
    oa, ob, oc, ga, gb, gc, g_scales, g_shifts, g_mix_a, g_mix_b, g_mix_c, g_patch, g_in, g_bias, g_out,
    wide_in, wide_out, square, copy_sem, out_sem,
):
    chans, chunks = plan.chans, plan.chunks
    moves = []
    for place, (source, target) in enumerate(zip((ia, ib, ic, ja, jb, jc), (oa, ob, oc, ga, gb, gc))):
        moves.append(pltpu.make_async_copy(source, target, copy_sem.at[place]))
    g_patch[...] = jnp.zeros_like(g_patch)
    for layer in reversed(range(LAYERS)):
        if layer == 0:
            for move in moves[:6]:
                move.start()
        first = (LAYERS - 1 - layer) * plan.steps
        for step in range(chunks):
            lanes = pl.ds(step * CHUNK, CHUNK)
            for part in range(CHUNK // LANES):
                spot = pl.ds(step * CHUNK + part * LANES, LANES)
                wide_in[layer, :, spot] = held[first + step, pl.ds(part * chans, chans), :].astype(f32)
            for part in range(chans // LANES):
                spot = pl.ds(part * LANES, LANES)
                wide_out[layer, lanes, spot] = held[first + step, pl.ds(plan.half + part * CHUNK, CHUNK), :].astype(f32)
            for place, (source, target) in enumerate(
                ((wide_in.at[layer, :, lanes], g_in.at[layer, :, lanes]), (wide_out.at[layer, lanes], g_out.at[layer, lanes]))
            ):
                moves.append(pltpu.make_async_copy(source, target, out_sem.at[layer, step, place]))
                moves[-1].start()
        offset = 0
        for kind, target in enumerate((g_mix_a, g_mix_b, g_mix_c)):
            width, rows_k, size = plan.widths[kind], plan.padded[kind], plan.wide[kind]
            for part in range(size // LANES):
                place = plan.places[kind] + part * rows_k
                square[0:rows_k, part * LANES : (part + 1) * LANES] = held[first + chunks, pl.ds(place, rows_k), :].astype(
                    f32
                )
            whole = square[0:rows_k, 0:size]
            target[:, layer, :] = whole[0:width, 0:width]
            row = lax.broadcasted_iota(jnp.int32, (rows_k, size), 0)
            col = lax.broadcasted_iota(jnp.int32, (rows_k, size), 1)
            column = jnp.sum(jnp.where(col == width, whole, 0.0), axis=1, keepdims=True)
            turned = jnp.sum(jnp.where((row == col) & (row < width), column, 0.0), axis=0, keepdims=True)
            g_patch[layer : layer + 1, offset : offset + width] = turned[:, 0:width]
            offset += width
        small = square[width : width + 7 + plan.hid // chans, :]
        for place, row in enumerate((0, 2, 3, 5)):
            g_scales[layer, place : place + 1, :] = small[row : row + 1]
        for place, row in enumerate((1, 4, 6)):
            g_shifts[place, layer : layer + 1, :] = small[row : row + 1]
        for place in range(plan.hid // chans):
            g_bias[layer : layer + 1, place * chans : (place + 1) * chans] = small[7 + place : 8 + place]
    for move in moves:
        move.wait()


def solution(mesh):
    sections, dp = mesh.shape["section"], mesh.shape["dp"]

    def run(*args):
        images, weight_in = args[:3], args[13]
        slots = images[0].shape[0] // (sections * dp)
        widths = tuple(image.shape[1] for image in images)
        plan = Plan(sections, dp, slots, widths, weight_in.shape[1], weight_in.shape[2])
        split_in = P("dp", None, None)
        split_out = P(("dp", "section"), None, None)
        in_specs = (split_in,) * 6 + (P("dp", None),) + (P(),) * 9
        out_specs = (split_out,) * 6 + (P(),) * 9
        whole = jax.shard_map(
            functools.partial(body, plan), mesh=mesh, in_specs=in_specs, out_specs=out_specs, check_vma=False
        )
        return whole(*args)

    return run
```
